256 devices in a mesh: replica: 4 (over y_lo, core), fsdp: 64 (over z, y_hi, x).
Axes of the slice: x: 4, y: 4 (y_hi: 2, y_lo: 2; y = y_hi * 2 + y_lo), z: 8, core: 2. Of those that a mesh axis runs over, the one named last changes fastest.
Arguments:
- local_weights: bfloat16 [4, 8192, 8192], P('replica', 'fsdp'), may hold values from -6 to 6
- anchor: bfloat16 [8192, 8192], P('fsdp'), may hold values from -6 to 6
- momentum: float32 [8192, 8192], P('replica', 'fsdp'), may hold values from -4 to 4
Outputs:
- new_momentum: float32 [8192, 8192], P('replica', 'fsdp')
- new_anchor: bfloat16 [8192, 8192], P('fsdp')
- mixed: bfloat16 [4, 8192, 8192], P('replica', 'fsdp')
The draws below stay inside these ranges and needn't reach their ends.
All inputs are finite; a program needn't handle non-finite values.
Results may differ from the reference program's by a relative error of at most 0.03.
Values may be sent and summed in bfloat16 or wider, within the bound.
No kernel may reach another device: no remote copies, remote signals or barrier semaphores. Data moves between devices by JAX's collectives and lax.ppermute only.
A program may use at most 64 MiB of HBM per device.

```python
import jax
import jax.numpy as jnp

D = 8192
ROWS = 8192
N_REPLICA = 4


def level_of(own_key, dims, pieces, smallest, high):
    level = 1.0
    for dim, blocks in pieces:
        steps = jax.random.uniform(jax.random.fold_in(jax.random.fold_in(own_key, 6), dim), (blocks,), jnp.float32, smallest / len(pieces), high / len(pieces))
        level = level * jnp.repeat(jnp.exp(steps), dims[dim] // blocks).reshape((-1,) + (1,) * (len(dims) - 1 - dim))
    return level


def bell_draw(key, shape, width, most, shards=(), dtype=jnp.bfloat16):
    loudness = level_of(key, shape, shards, -0.22, 0.18) if shards else 1.0
    result = jax.random.normal(key, shape, jnp.float32) * width * loudness
    return jnp.minimum(jnp.maximum(result, -most), most).astype(dtype)


def setup_inputs(seed: int = 0) -> dict:
    key_list = jax.random.split(jax.random.key(seed), 4)
    return {
        "local_weights": bell_draw(key_list[0], (N_REPLICA, ROWS, D), 1.0, 6.0, ((0, 4), (1, 64))),
        "anchor": bell_draw(key_list[1], (ROWS, D), 1.0, 6.0, ((0, 64),)),
        "momentum": bell_draw(key_list[2], (ROWS, D), 0.5, 4.0, ((0, 4), (1, 64)), jnp.float32),
    }


outer_rate = 0.7
outer_beta = 0.9
mix_weight = 0.5


def reference(local_weights, anchor, momentum):
    anchor_wide = anchor.astype(jnp.float32)
    local_wide = local_weights.astype(jnp.float32)
    delta = (anchor_wide[None] - local_wide).astype(jnp.bfloat16)
    average = jnp.sum(delta.astype(jnp.float32), axis=0) / N_REPLICA
    new_momentum = outer_beta * momentum + average
    change = (outer_rate * (average + outer_beta * new_momentum)).astype(jnp.bfloat16)
    global_new = anchor_wide - change.astype(jnp.float32)
    new_anchor = global_new.astype(jnp.bfloat16)
    mixed = (mix_weight * local_wide + (1.0 - mix_weight) * global_new[None]).astype(jnp.bfloat16)
    return new_momentum, new_anchor, mixed
```

```python
import functools

import jax
import jax.numpy as jnp
from jax import lax
from jax.experimental import pallas as pl
from jax.experimental.pallas import tpu as pltpu
from jax.sharding import PartitionSpec as P

outer_rate = 0.7
outer_beta = 0.9
mix_weight = 0.5

BF = jnp.bfloat16
F32 = jnp.float32


def seg_of(r):
    return 2 * (r % 2) + r // 2


def params(mib=48):
    return pltpu.CompilerParams(vmem_limit_bytes=mib * 2**20)


def cost(n):
    return pl.CostEstimate(flops=n // 2, bytes_accessed=n, transcendentals=0)


def swap(x, k):
    return lax.ppermute(x, "replica", [(i, i ^ k) for i in range(4)])


def split_momentum(r, momentum):
    def body(r_ref, m_ref, *outs):
        for k in range(4):
            seg = seg_of(jnp.bitwise_xor(r_ref[0], k))
            for j in range(16):
                at = pl.multiple_of(j * 128 + seg * 32, 32)
                outs[k][j] = m_ref[pl.ds(at, 32), :].astype(BF)

    return pl.pallas_call(
        body,
        out_shape=[jax.ShapeDtypeStruct((16, 32, 128), BF)] * 4,
        in_specs=[pl.BlockSpec(memory_space=pltpu.SMEM), pl.BlockSpec(memory_space=pltpu.VMEM)],
        out_specs=[pl.BlockSpec(memory_space=pltpu.VMEM)] * 4,
        compiler_params=params(),
        cost_estimate=cost(3 << 19),
        name="split_momentum",
    )(r, momentum)


def in_order(r, pieces):
    def body(r_ref, *refs):
        for k in range(4):
            refs[4][jnp.bitwise_xor(r_ref[0], k)] = refs[k][...]

    return pl.pallas_call(
        body,
        out_shape=jax.ShapeDtypeStruct((4, 16, 32, 128), BF),
        in_specs=[pl.BlockSpec(memory_space=pltpu.SMEM)] + [pl.BlockSpec(memory_space=pltpu.VMEM)] * 4,
        out_specs=pl.BlockSpec(memory_space=pltpu.VMEM),
        compiler_params=params(),
        cost_estimate=cost(1 << 20),
        name="in_order",
    )(r, *pieces)


def out_of_order(r, whole):
    def body(r_ref, x_ref, *outs):
        for k in range(4):
            outs[k][...] = x_ref[jnp.bitwise_xor(r_ref[0], k)]

    return pl.pallas_call(
        body,
        out_shape=[jax.ShapeDtypeStruct((16, 32, 128), BF)] * 4,
        in_specs=[pl.BlockSpec(memory_space=pltpu.SMEM), pl.BlockSpec(memory_space=pltpu.VMEM)],
        out_specs=[pl.BlockSpec(memory_space=pltpu.VMEM)] * 4,
        compiler_params=params(),
        cost_estimate=cost(1 << 20),
        name="out_of_order",
    )(r, whole)


WIDTH = 2048


def spec(row):
    return pl.BlockSpec((32, WIDTH), lambda i, s: (row(s[0]), i))


def partial_for_other(r, local, theirs, anchor):
    def body(s_ref, l_ref, t_ref, a_ref, o_ref):
        a = a_ref[...].astype(F32)
        o_ref[...] = ((a - l_ref[...].astype(F32)) + (a - t_ref[...].astype(F32))).astype(BF)

    other = lambda r: seg_of(jnp.bitwise_xor(r, 2))
    return pl.pallas_call(
        body,
        out_shape=jax.ShapeDtypeStruct((32, 8192), BF),
        grid_spec=pltpu.PrefetchScalarGridSpec(
            num_scalar_prefetch=1,
            grid=(8192 // WIDTH,),
            in_specs=[spec(other), spec(lambda r: 1 - r // 2), spec(other)],
            out_specs=pl.BlockSpec((32, WIDTH), lambda i, s: (0, i)),
        ),
        compiler_params=params(),
        cost_estimate=cost(1 << 21),
        name="partial_for_other",
    )(r, local, theirs, anchor)


def average_rows(r, local, theirs, anchor, partial):
    def body(s_ref, l_ref, t_ref, a_ref, p_ref, avg_ref, cut_ref):
        a = a_ref[...].astype(F32)
        own = (a - l_ref[...].astype(F32)) + (a - t_ref[...].astype(F32))
        avg = (own + p_ref[...].astype(F32)) * 0.25
        avg_ref[...] = avg
        narrow = avg.astype(BF)
        for i in range(WIDTH // 128):
            cut_ref[i] = narrow[:, i * 128 : (i + 1) * 128]

    return pl.pallas_call(
        body,
        out_shape=[
            jax.ShapeDtypeStruct((32, 8192), F32),
            jax.ShapeDtypeStruct((64, 32, 128), BF),
        ],
        grid_spec=pltpu.PrefetchScalarGridSpec(
            num_scalar_prefetch=1,
            grid=(8192 // WIDTH,),
            in_specs=[
                spec(seg_of),
                spec(lambda r: r // 2),
                spec(seg_of),
                pl.BlockSpec((32, WIDTH), lambda i, s: (0, i)),
            ],
            out_specs=[
                pl.BlockSpec((32, WIDTH), lambda i, s: (0, i)),
                pl.BlockSpec((WIDTH // 128, 32, 128), lambda i, s: (i, 0, 0)),
            ],
        ),
        compiler_params=params(),
        cost_estimate=cost(4 << 20),
        name="average_rows",
    )(r, local, theirs, anchor, partial)


def change_rows(avg, m):
    def body(avg_ref, m_ref, o_ref):
        for i in range(WIDTH // 128):
            at = slice(i * 128, (i + 1) * 128)
            average = avg_ref[:, at]
            momentum = outer_beta * m_ref[i].astype(F32) + average
            o_ref[:, at] = (outer_rate * (average + outer_beta * momentum)).astype(BF)

    return pl.pallas_call(
        body,
        out_shape=jax.ShapeDtypeStruct((32, 8192), BF),
        grid=(8192 // WIDTH,),
        in_specs=[
            pl.BlockSpec((32, WIDTH), lambda i: (0, i)),
            pl.BlockSpec((WIDTH // 128, 32, 128), lambda i: (i, 0, 0)),
        ],
        out_specs=pl.BlockSpec((32, WIDTH), lambda i: (0, i)),
        compiler_params=params(),
        cost_estimate=cost(2 << 20),
        name="change_rows",
    )(avg, m)


def new_momentum_of(r, momentum, pieces):
    def body(r_ref, m_ref, *refs):
        for k in range(4):
            seg = seg_of(jnp.bitwise_xor(r_ref[0], k))
            for j in range(16):
                at = pl.ds(pl.multiple_of(j * 128 + seg * 32, 32), 32)
                refs[4][at, :] = outer_beta * m_ref[at, :] + refs[k][j].astype(F32)

    return pl.pallas_call(
        body,
        out_shape=jax.ShapeDtypeStruct((2048, 128), F32),
        in_specs=[pl.BlockSpec(memory_space=pltpu.SMEM)] + [pl.BlockSpec(memory_space=pltpu.VMEM)] * 5,
        out_specs=pl.BlockSpec(memory_space=pltpu.VMEM),
        compiler_params=params(),
        cost_estimate=cost(5 << 19),
        name="new_momentum_of",
    )(r, momentum, *pieces)


def outputs_of(r, local, anchor, changes):
    width = 1024

    def body(r_ref, l_ref, a_ref, *refs):
        new_ref, mixed_ref = refs[4:]
        for k in range(4):
            seg = seg_of(jnp.bitwise_xor(r_ref[0], k))
            at = pl.ds(pl.multiple_of(seg * 32, 32), 32)
            global_new = a_ref[at, :].astype(F32) - refs[k][...].astype(F32)
            new_ref[at, :] = global_new.astype(BF)
            mixed_ref[at, :] = (
                mix_weight * l_ref[at, :].astype(F32) + (1.0 - mix_weight) * global_new
            ).astype(BF)

    tall = pl.BlockSpec((128, width), lambda i, s: (0, i))
    flat = pl.BlockSpec((32, width), lambda i, s: (0, i))
    return pl.pallas_call(
        body,
        out_shape=[jax.ShapeDtypeStruct((128, 8192), BF)] * 2,
        grid_spec=pltpu.PrefetchScalarGridSpec(
            num_scalar_prefetch=1,
            grid=(8192 // width,),
            in_specs=[tall, tall] + [flat] * 4,
            out_specs=[tall, tall],
        ),
        compiler_params=params(),
        cost_estimate=cost(10 << 20),
        name="outputs_of",
    )(r, local, anchor, *changes)


def local(local_weights, anchor, momentum):
    own = local_weights[0]
    me = lax.axis_index("replica")
    r = me[None].astype(jnp.int32)
    core = me % 2

    theirs = swap(lax.dynamic_slice_in_dim(own, (1 - core) * 64, 64, 0), 1)

    pieces = split_momentum(r, momentum)
    pieces = [pieces[0]] + [swap(pieces[k], k) for k in (1, 2, 3)]
    by_row = in_order(r, pieces).reshape(64, 32, 128)
    m_rows = lax.all_to_all(by_row, "fsdp", 0, 0, tiled=True)

    partial = swap(partial_for_other(r, own, theirs, anchor), 2)
    avg, cut = average_rows(r, own, theirs, anchor, partial)

    cut = lax.all_to_all(cut, "fsdp", 0, 0, tiled=True).reshape(4, 16, 32, 128)
    cut = out_of_order(r, cut)
    cut = [cut[0]] + [swap(cut[k], k) for k in (1, 2, 3)]
    new_momentum = new_momentum_of(r, momentum, cut)

    change = change_rows(avg, m_rows)
    change2 = swap(change, 2)
    change1 = swap(change, 1)
    change3 = swap(change2, 1)
    new_anchor, mixed = outputs_of(r, own, anchor, [change, change1, change2, change3])
    return new_momentum, new_anchor, mixed[None]


def solution(mesh):
    return jax.shard_map(
        local,
        mesh=mesh,
        in_specs=(P("replica", "fsdp", None), P("fsdp", None), P("replica", "fsdp")),
        out_specs=(P("replica", "fsdp"), P("fsdp", None), P("replica", "fsdp", None)),
        check_vma=False,
    )
```

```python
import jax
import jax.numpy as jnp
from jax import lax
from jax.experimental import pallas as pl
from jax.experimental.pallas import tpu as pltpu
from jax.sharding import PartitionSpec as P

outer_rate = 0.7
outer_beta = 0.9
mix_weight = 0.5

BF = jnp.bfloat16
F32 = jnp.float32
VM = pl.BlockSpec(memory_space=pltpu.VMEM)
SM = pl.BlockSpec(memory_space=pltpu.SMEM)
HBM = pl.BlockSpec(memory_space=pltpu.HBM)
ANY = pl.BlockSpec(memory_space=pl.ANY)
STEP = 1024
ORDER = 1 << 34
AVERAGE = 1 << 34
OUTPUTS = 2 << 20


def seg_of(r):
    return 2 * (r % 2) + r // 2


def peer(r, k):
    return jnp.bitwise_xor(r, k)


def shape(*dims, dtype=BF):
    return jax.ShapeDtypeStruct(dims, dtype)


def rows(start, count):
    return pl.ds(pl.multiple_of(start, count), count)


def call(body, name, nbytes, out_shape, in_specs, out_specs, **more):
    return pl.pallas_call(
        body,
        out_shape=out_shape,
        in_specs=in_specs,
        out_specs=out_specs,
        compiler_params=pltpu.CompilerParams(vmem_limit_bytes=12 * 2**20),
        cost_estimate=pl.CostEstimate(flops=nbytes, bytes_accessed=nbytes, transcendentals=0),
        name=name,
        **more,
    )


def swap(x, k):
    return lax.ppermute(x, "replica", [(i, i ^ k) for i in range(4)])


def half_for_core(r, local):
    def body(r_ref, l_ref, o_ref, sem):
        at = rows((1 - r_ref[0] % 2) * 64, 64)
        copy = pltpu.make_async_copy(l_ref.at[at, :], o_ref, sem)
        copy.start()
        copy.wait()

    return call(
        body, "half_for_core", 2 << 20, shape(64, 8192), [SM, HBM], VM,
        scratch_shapes=[pltpu.SemaphoreType.DMA],
    )(r, local)


def split_momentum(r, momentum):
    def body(r_ref, m_ref, *outs):
        for k in range(4):
            seg = seg_of(peer(r_ref[0], k))
            for j in range(16):
                outs[k][j] = m_ref[rows(j * 128 + seg * 32, 32), :].astype(BF)

    return call(
        body, "split_momentum", 3 << 19, [shape(16, 32, 128)] * 4, [SM, VM], [VM] * 4
    )(r, momentum)


def in_order(r, pieces, after):
    def body(r_ref, *refs):
        for k in range(4):
            refs[5][peer(r_ref[0], k)] = refs[k][...]

    return call(
        body, "in_order", ORDER, shape(4, 16, 32, 128), [SM] + [VM] * 4 + [ANY], VM
    )(r, *pieces, after)


def partial_for_other(r, local, theirs, anchor, after):
    def body(r_ref, l_ref, t_ref, a_ref, after_ref, o_ref):
        at = rows(seg_of(peer(r_ref[0], 2)) * 32, 32)
        half = rows((1 - r_ref[0] // 2) * 32, 32)

        def step(i, carry):
            cols = rows(i * STEP, STEP)
            a = a_ref[at, cols].astype(F32)
            mine = a - l_ref[at, cols].astype(F32)
            o_ref[:, cols] = (mine + (a - t_ref[half, cols].astype(F32))).astype(BF)
            return carry

        lax.fori_loop(0, 8192 // STEP, step, 0)

    return call(
        body, "partial_for_other", 2 << 20, shape(32, 8192), [SM, VM, VM, VM, ANY], VM
    )(r, local, theirs, anchor, after)


def average_rows(r, local, theirs, anchor, partial):
    def body(r_ref, l_ref, t_ref, a_ref, p_ref, avg_ref):
        at = rows(seg_of(r_ref[0]) * 32, 32)
        half = rows((r_ref[0] // 2) * 32, 32)

        def step(i, carry):
            cols = rows(i * STEP, STEP)
            a = a_ref[at, cols].astype(F32)
            own = (a - l_ref[at, cols].astype(F32)) + (a - t_ref[half, cols].astype(F32))
            avg_ref[:, cols] = (own + p_ref[:, cols].astype(F32)) * 0.25
            return carry

        lax.fori_loop(0, 8192 // STEP, step, 0)

    return call(
        body, "average_rows", AVERAGE, shape(32, 8192, dtype=F32), [SM] + [VM] * 4, VM
    )(r, local, theirs, anchor, partial)


def cut_columns(r, avg):
    def body(r_ref, avg_ref, *outs):
        for k in range(4):
            start = peer(r_ref[0], k) * 2048

            def step(n, carry):
                outs[k][n] = avg_ref[:, rows(start + n * 128, 128)].astype(BF)
                return carry

            lax.fori_loop(0, 16, step, 0, unroll=8)

    return call(
        body, "cut_columns", 3 << 19, [shape(16, 32, 128)] * 4, [SM, VM], [VM] * 4
    )(r, avg)


def stack_pieces(pieces):
    def body(*refs):
        for k in range(4):
            refs[4][:, k] = refs[k][...]

    return call(body, "stack_pieces", 1 << 20, shape(16, 4, 32, 128), [VM] * 4, VM)(*pieces)


def change_rows(avg, m):
    def body(avg_ref, m_ref, o_ref):
        def step(n, carry):
            cols = rows(n * 128, 128)
            average = avg_ref[:, cols]
            momentum = outer_beta * m_ref[n].astype(F32) + average
            o_ref[:, cols] = (outer_rate * (average + outer_beta * momentum)).astype(BF)
            return carry

        lax.fori_loop(0, 64, step, 0, unroll=8)

    return call(body, "change_rows", 2 << 20, shape(32, 8192), [VM, VM], VM)(avg, m)


def new_momentum_of(g, momentum, pieces):
    def body(g_ref, m_ref, p_ref, o_ref):
        for k in range(4):
            seg = seg_of(peer(g_ref[0], k))
            for j in range(16):
                at = rows(j * 128 + seg * 32, 32)
                o_ref[at, :] = outer_beta * m_ref[at, :] + p_ref[j, k].astype(F32)

    return call(
        body, "new_momentum_of", 5 << 19, shape(2048, 128, dtype=F32), [SM, VM, VM], VM
    )(g, momentum, pieces)


def outputs_of(r, local, anchor, changes, before):
    ks = sorted(changes)
    n = len(ks)
    parts, width = 4, 2048

    def body(r_ref, l_ref, a_ref, *refs):
        news, mixes, sems = refs[-3:]
        new_ref, mixed_ref = refs[-5:-3]
        copies = []
        for m, k in enumerate(ks):
            at = rows(seg_of(peer(r_ref[0], k)) * 32, 32)
            for p in range(parts):

                def step(i, carry, m=m, p=p, at=at):
                    cols = rows(p * width + i * 512, 512)
                    global_new = a_ref[at, cols].astype(F32) - refs[m][:, cols].astype(F32)
                    news[m, :, cols] = global_new.astype(BF)
                    mixes[m, :, cols] = (
                        mix_weight * l_ref[at, cols].astype(F32) + (1.0 - mix_weight) * global_new
                    ).astype(BF)
                    return carry

                lax.fori_loop(0, width // 512, step, 0)
                cols = pl.ds(p * width, width)
                for o, (src, dst) in enumerate(((news, new_ref), (mixes, mixed_ref))):
                    sem = sems.at[(m * parts + p) * 2 + o]
                    copy = pltpu.make_async_copy(src.at[m, :, cols], dst.at[at, cols], sem)
                    copy.start()
                    copies.append(copy)
        for copy in copies:
            copy.wait()

    return call(
        body, "outputs_of", OUTPUTS, [shape(128, 8192)] * 2,
        [SM] + [VM] * (2 + n) + [HBM] * len(before), [HBM, HBM],
        scratch_shapes=[
            pltpu.VMEM((n, 32, 8192), BF),
            pltpu.VMEM((n, 32, 8192), BF),
            pltpu.SemaphoreType.DMA((n * parts * 2,)),
        ],
        input_output_aliases={3 + n + b: b for b in range(len(before))},
    )(r, local, anchor, *[changes[k] for k in ks], *before)


def across(x, k):
    pairs = [
        (64 * r + 16 * g + q, 64 * g + 16 * (r ^ k) + q)
        for r in range(4)
        for g in range(4)
        for q in range(16)
    ]
    return lax.ppermute(x, ("replica", "fsdp"), pairs)


def local(local_weights, anchor, momentum):
    own = local_weights[0]
    r = lax.axis_index("replica")[None].astype(jnp.int32)
    g = (lax.axis_index("fsdp") // 16)[None].astype(jnp.int32)

    theirs = swap(half_for_core(r, own), 1)

    pieces = split_momentum(r, momentum)
    head = pieces[0]
    pieces = [head] + [swap(pieces[k], k) for k in (1, 2, 3)]
    for_other = partial_for_other(r, own, theirs, anchor, head)
    partial = swap(for_other, 2)
    by_row = in_order(r, pieces, for_other).reshape(64, 32, 128)
    m_rows = lax.all_to_all(by_row, "fsdp", 0, 0, tiled=True)

    avg = average_rows(r, own, theirs, anchor, partial)
    cut = stack_pieces([across(x, k) for k, x in enumerate(cut_columns(r, avg))])
    groups = [[16 * i + q for q in range(16)] for i in range(4)]
    cut = lax.all_to_all(cut, "fsdp", 0, 0, axis_index_groups=groups, tiled=True)
    new_momentum = new_momentum_of(g, momentum, cut)

    change = change_rows(avg, m_rows)
    change2 = swap(change, 2)
    change1 = swap(change, 1)
    change3 = swap(change2, 1)
    outs = outputs_of(r, own, anchor, {0: change, 1: change1}, ())
    outs = outputs_of(r, own, anchor, {2: change2}, outs)
    new_anchor, mixed = outputs_of(r, own, anchor, {3: change3}, outs)
    return new_momentum, new_anchor, mixed[None]


def solution(mesh):
    return jax.shard_map(
        local,
        mesh=mesh,
        in_specs=(P("replica", "fsdp", None), P("fsdp", None), P("replica", "fsdp")),
        out_specs=(P("replica", "fsdp"), P("fsdp", None), P("replica", "fsdp", None)),
        check_vma=False,
    )
```

```python
import jax
import jax.numpy as jnp
from jax import lax
from jax.experimental import pallas as pl
from jax.experimental.pallas import tpu as pltpu
from jax.sharding import PartitionSpec as P

outer_rate = 0.7
outer_beta = 0.9
mix_weight = 0.5

BF = jnp.bfloat16
F32 = jnp.float32
PARTS = 4
WIDTH = 8192 // PARTS
INNER = 512
SHORT = 2 << 20
LONG = 1 << 34
VMEM_MIB = 16


def seg_of(r):
    return 2 * (r % 2) + r // 2


def peer(r, k):
    return jnp.bitwise_xor(r, k)


def shape(*dims, dtype=BF):
    return jax.ShapeDtypeStruct(dims, dtype)


def at(start, count):
    return pl.ds(pl.multiple_of(start, count), count)


class Copies:
    def __init__(self, sems):
        self.sems, self.count, self.open = sems, 0, []

    def start(self, src, dst):
        copy = pltpu.make_async_copy(src, dst, self.sems.at[self.count])
        copy.start()
        self.count += 1
        return copy

    def send(self, src, dst):
        self.open.append(self.start(src, dst))

    def finish(self):
        for copy in self.open:
            copy.wait()


def call(body, name, cost, outs, args, scratch, copies, aliases=None, near=None, out_near=False):
    anywhere = pl.BlockSpec(memory_space=pl.ANY)
    whole = pl.BlockSpec(memory_space=pltpu.VMEM)
    near = len(args) if near is None else near
    out_spec = whole if out_near else anywhere
    single = not isinstance(outs, list)
    count = 1 if single else len(outs)
    return pl.pallas_call(
        body,
        out_shape=outs,
        in_specs=[pl.BlockSpec(memory_space=pltpu.SMEM)]
        + [anywhere] * (near - 1)
        + [whole] * (len(args) - near),
        out_specs=out_spec if single else [out_spec] * count,
        scratch_shapes=[pltpu.VMEM(x.shape, x.dtype) for x in scratch]
        + [pltpu.SemaphoreType.DMA((copies,))],
        input_output_aliases=aliases or {},
        compiler_params=pltpu.CompilerParams(vmem_limit_bytes=VMEM_MIB * 2**20),
        cost_estimate=pl.CostEstimate(flops=cost, bytes_accessed=cost, transcendentals=0),
        name=name,
    )(*args)


def swap(x, k):
    return lax.ppermute(x, "replica", [(i, i ^ k) for i in range(4)])


def swap_around(x):
    pairs = [(64 * i + f, 64 * (i ^ 3) + (f ^ 4)) for i in range(4) for f in range(64)]
    return lax.ppermute(x, ("replica", "fsdp"), pairs)


def prologue(r, local, momentum):
    def body(r_ref, l_ref, m_ref, half_ref, *refs):
        outs, (m, sems) = refs[:4], refs[4:]
        copies = Copies(sems)
        loads = [
            copies.start(m_ref.at[pl.ds(p * 512, 512), :], m.at[pl.ds(p * 512, 512), :])
            for p in range(4)
        ]
        other = 1 - r_ref[0] % 2
        copies.send(l_ref.at[at(other * 64, 64), :], half_ref)
        for p in range(4):
            loads[p].wait()
            for k in range(4):
                seg = seg_of(peer(r_ref[0], k))
                for j in range(4 * p, 4 * p + 4):
                    outs[k][j] = m[at(j * 128 + seg * 32, 32), :].astype(BF)
        copies.finish()

    return call(
        body, "prologue", SHORT, [shape(64, 8192)] + [shape(16, 32, 128)] * 4,
        [r, local, momentum], [shape(2048, 128, dtype=F32)], 5, out_near=True,
    )


def in_order(r, pieces, after):
    def body(r_ref, after_ref, *refs):
        for k in range(4):
            refs[4][peer(r_ref[0], k)] = refs[k][...]

    return call(
        body, "in_order", LONG, shape(4, 16, 32, 128), [r, after, *pieces], [], 1,
        near=2, out_near=True,
    )


def inner(step):
    lax.fori_loop(0, WIDTH // INNER, lambda i, c: (step(at(i * INNER, INNER)), c)[1], 0)


def partial_for_other(r, local, theirs, anchor, after):
    def body(r_ref, l_ref, t_ref, a_ref, after_ref, o_ref, l, t, a, o, sems):
        mine = at(seg_of(peer(r_ref[0], 2)) * 32, 32)
        half = at((1 - r_ref[0] // 2) * 32, 32)
        copies = Copies(sems)
        loads = []
        for p in range(PARTS):
            cols = pl.ds(p * WIDTH, WIDTH)
            loads.append([
                copies.start(l_ref.at[mine, cols], l.at[p]),
                copies.start(t_ref.at[half, cols], t.at[p]),
                copies.start(a_ref.at[mine, cols], a.at[p]),
            ])
        for p in range(PARTS):
            for load in loads[p]:
                load.wait()

            def step(cols, p=p):
                x = a[p, :, cols].astype(F32)
                total = (x - l[p, :, cols].astype(F32)) + (x - t[p, :, cols].astype(F32))
                o[p, :, cols] = total.astype(BF)

            inner(step)
            copies.send(o.at[p], o_ref.at[:, pl.ds(p * WIDTH, WIDTH)])
        copies.finish()

    return call(
        body, "partial_for_other", SHORT, shape(32, 8192), [r, local, theirs, anchor, after],
        [shape(PARTS, 32, WIDTH)] * 4, 4 * PARTS,
    )


def average_rows(r, local, theirs, anchor, partial):
    def body(r_ref, l_ref, t_ref, a_ref, p_ref, avg_ref, *refs):
        outs, (l, t, a, q, avg, cut, sems) = refs[:4], refs[4:]
        mine = at(seg_of(r_ref[0]) * 32, 32)
        half = at((r_ref[0] // 2) * 32, 32)
        copies = Copies(sems)
        loads = []
        for k in range(4):
            cols = at(peer(r_ref[0], k) * WIDTH, WIDTH)
            loads.append([
                copies.start(l_ref.at[mine, cols], l.at[k]),
                copies.start(t_ref.at[half, cols], t.at[k]),
                copies.start(a_ref.at[mine, cols], a.at[k]),
                copies.start(p_ref.at[:, cols], q.at[k]),
            ])
        for k in range(4):
            for load in loads[k]:
                load.wait()

            def step(i, carry, k=k):
                cols = at(i * INNER, INNER)
                x = a[k, :, cols].astype(F32)
                own = (x - l[k, :, cols].astype(F32)) + (x - t[k, :, cols].astype(F32))
                y = (own + q[k, :, cols].astype(F32)) * 0.25
                avg[k, :, cols] = y
                narrow = y.astype(BF)
                for n in range(INNER // 128):
                    cut[k, i * (INNER // 128) + n] = narrow[:, n * 128 : (n + 1) * 128]
                return carry

            lax.fori_loop(0, WIDTH // INNER, step, 0)
            copies.send(cut.at[k], outs[k])
            copies.send(avg.at[k], avg_ref.at[:, at(peer(r_ref[0], k) * WIDTH, WIDTH)])
        copies.finish()

    return call(
        body, "average_rows", LONG, [shape(32, 8192, dtype=F32)] + [shape(16, 32, 128)] * 4,
        [r, local, theirs, anchor, partial],
        [shape(4, 32, WIDTH)] * 4 + [shape(4, 32, WIDTH, dtype=F32), shape(4, 16, 32, 128)], 24,
    )


def stack_pieces(r, pieces):
    def body(r_ref, *refs):
        for k in range(4):
            refs[4][:, k] = refs[k][...]

    return call(
        body, "stack_pieces", SHORT, shape(16, 4, 32, 128), [r, *pieces], [], 1,
        near=1, out_near=True,
    )


def change_rows(rg, average, m_rows):
    def body(rg_ref, avg_ref, m_ref, o_ref, avg, m, o, sems):
        flip = jnp.where(peer(rg_ref[0], rg_ref[1]) == 3, 4, 0)
        copies = Copies(sems)
        loads = [
            (
                copies.start(avg_ref.at[:, pl.ds(p * WIDTH, WIDTH)], avg.at[p]),
                copies.start(m_ref.at[pl.ds(p * 16, 16)], m.at[p]),
            )
            for p in range(PARTS)
        ]
        for p in range(PARTS):
            for load in loads[p]:
                load.wait()

            def step(n, carry, p=p):
                cols = at(n * 128, 128)
                x = avg[p, :, cols]
                momentum = outer_beta * m[p, peer(n, flip)].astype(F32) + x
                o[p, :, cols] = (outer_rate * (x + outer_beta * momentum)).astype(BF)
                return carry

            lax.fori_loop(0, 16, step, 0, unroll=4)
            copies.send(o.at[p], o_ref.at[:, pl.ds(p * WIDTH, WIDTH)])
        copies.finish()

    return call(
        body, "change_rows", SHORT, shape(32, 8192), [rg, average, m_rows],
        [shape(PARTS, 32, WIDTH, dtype=F32), shape(4, 16, 32, 128), shape(PARTS, 32, WIDTH)],
        3 * PARTS,
    )


def new_momentum_of(rg, momentum, pieces, after):
    def body(rg_ref, after_ref, p_ref, m_ref, o_ref, q, o, sems):
        copies = Copies(sems)
        copies.send(p_ref, q)
        copies.finish()
        copies.open = []
        r, g = rg_ref[0], rg_ref[1]
        for p in range(4):
            for k in range(4):
                other = peer(g, k)
                flip = jnp.where(other // 2 == r // 2, 0, 4)
                for j in range(4):
                    rows = at(j * 128 + seg_of(other) * 32, 32)
                    all_rows = at((4 * p + j) * 128 + seg_of(other) * 32, 32)
                    piece = q[peer(4 * p + j, flip), k].astype(F32)
                    o[p, rows, :] = outer_beta * m_ref[all_rows, :] + piece
            copies.send(o.at[p], o_ref.at[pl.ds(p * 512, 512), :])
        copies.finish()

    return call(
        body, "new_momentum_of", SHORT, shape(2048, 128, dtype=F32),
        [rg, after, pieces, momentum], [shape(16, 4, 32, 128), shape(4, 512, 128, dtype=F32)], 5,
        near=3,
    )


def outputs_of(r, local, anchor, changes, before):
    ks = sorted(changes)
    n = len(ks)

    def body(r_ref, l_ref, a_ref, *refs):
        new_ref, mixed_ref, l, a, c, new, mixed, sems = refs[-8:]
        copies = Copies(sems)
        loads = []
        for m, k in enumerate(ks):
            rows = at(seg_of(peer(r_ref[0], k)) * 32, 32)
            for p in range(PARTS):
                cols = pl.ds(p * WIDTH, WIDTH)
                i = m * PARTS + p
                loads.append((
                    rows,
                    cols,
                    copies.start(l_ref.at[rows, cols], l.at[i]),
                    copies.start(a_ref.at[rows, cols], a.at[i]),
                    copies.start(refs[m].at[:, cols], c.at[i]),
                ))
        for i, (rows, cols, *waits) in enumerate(loads):
            for load in waits:
                load.wait()

            def step(x, i=i):
                global_new = a[i, :, x].astype(F32) - c[i, :, x].astype(F32)
                new[i, :, x] = global_new.astype(BF)
                mixed[i, :, x] = (
                    mix_weight * l[i, :, x].astype(F32) + (1.0 - mix_weight) * global_new
                ).astype(BF)

            inner(step)
            copies.send(new.at[i], new_ref.at[rows, cols])
            copies.send(mixed.at[i], mixed_ref.at[rows, cols])
        copies.finish()

    return call(
        body, "outputs_of", SHORT, [shape(128, 8192)] * 2,
        [r, local, anchor, *[changes[k] for k in ks], *before],
        [shape(n * PARTS, 32, WIDTH)] * 5, 5 * n * PARTS,
        {3 + n + b: b for b in range(len(before))},
    )


def across(x, k):
    pairs = [
        (64 * r + 16 * g + q, 64 * g + 16 * (r ^ k) + (q if r // 2 == g // 2 else q ^ 4))
        for r in range(4)
        for g in range(4)
        for q in range(16)
    ]
    return lax.ppermute(x, ("replica", "fsdp"), pairs)


def in_hbm(x):
    return pltpu.with_memory_space_constraint(x, pltpu.HBM)


def local(local_weights, anchor, momentum):
    own, anchor = in_hbm(local_weights[0]), in_hbm(anchor)
    r = lax.axis_index("replica")[None].astype(jnp.int32)
    g = (lax.axis_index("fsdp") // 16)[None].astype(jnp.int32)
    rg = jnp.concatenate([r, g])

    half, *pieces = prologue(r, own, in_hbm(momentum))
    theirs = swap(half, 1)
    pieces = [pieces[0], swap(pieces[1], 1), swap(pieces[2], 2), swap_around(pieces[3])]
    for_other = partial_for_other(r, own, theirs, anchor, pieces[0])
    partial = swap(for_other, 2)
    by_row = in_order(r, pieces, for_other).reshape(64, 32, 128)
    m_rows = lax.all_to_all(by_row, "fsdp", 0, 0, tiled=True)

    average, *cut = average_rows(r, own, theirs, anchor, in_hbm(partial))
    cut = stack_pieces(r, [across(x, k) for k, x in enumerate(cut)])
    groups = [[16 * i + q for q in range(16)] for i in range(4)]
    cut = lax.all_to_all(cut, "fsdp", 0, 0, axis_index_groups=groups, tiled=True)

    change = change_rows(rg, average, m_rows)
    change2 = swap(change, 2)
    change1 = swap(change, 1)
    change3 = swap(change2, 1)
    outs = outputs_of(r, own, anchor, {0: change, 1: change1}, ())
    outs = outputs_of(r, own, anchor, {2: change2}, outs)
    new_anchor, mixed = outputs_of(r, own, anchor, {3: change3}, outs)
    new_momentum = new_momentum_of(rg, momentum, cut, in_hbm(mixed))
    return new_momentum, new_anchor, mixed[None]


def solution(mesh):
    return jax.shard_map(
        local,
        mesh=mesh,
        in_specs=(P("replica", "fsdp", None), P("fsdp", None), P("replica", "fsdp")),
        out_specs=(P("replica", "fsdp"), P("fsdp", None), P("replica", "fsdp", None)),
        check_vma=False,
    )
```

```python
import jax
import jax.numpy as jnp
from jax import lax
from jax.experimental import pallas as pl
from jax.experimental.pallas import tpu as pltpu
from jax.sharding import PartitionSpec as P

outer_rate = 0.7
outer_beta = 0.9
mix_weight = 0.5

BF = jnp.bfloat16
F32 = jnp.float32
PARTS = 4
WIDTH = 8192 // PARTS
INNER = 512
SHORT = 2 << 20
LONG = 1 << 34
VMEM_MIB = 16


def seg_of(r):
    return 2 * (r % 2) + r // 2


def peer(r, k):
    return jnp.bitwise_xor(r, k)


def shape(*dims, dtype=BF):
    return jax.ShapeDtypeStruct(dims, dtype)


def at(start, count):
    return pl.ds(pl.multiple_of(start, count), count)


class Copies:
    def __init__(self, sems):
        self.sems, self.count, self.open = sems, 0, []

    def start(self, src, dst):
        copy = pltpu.make_async_copy(src, dst, self.sems.at[self.count])
        copy.start()
        self.count += 1
        return copy

    def send(self, src, dst):
        self.open.append(self.start(src, dst))

    def finish(self):
        for copy in self.open:
            copy.wait()


def call(body, name, cost, outs, args, scratch, copies, aliases=None, near=None, out_near=False):
    anywhere = pl.BlockSpec(memory_space=pl.ANY)
    whole = pl.BlockSpec(memory_space=pltpu.VMEM)
    near = len(args) if near is None else near
    out_spec = whole if out_near else anywhere
    single = not isinstance(outs, list)
    count = 1 if single else len(outs)
    return pl.pallas_call(
        body,
        out_shape=outs,
        in_specs=[pl.BlockSpec(memory_space=pltpu.SMEM)]
        + [anywhere] * (near - 1)
        + [whole] * (len(args) - near),
        out_specs=out_spec if single else [out_spec] * count,
        scratch_shapes=[pltpu.VMEM(x.shape, x.dtype) for x in scratch]
        + [pltpu.SemaphoreType.DMA((copies,))],
        input_output_aliases=aliases or {},
        compiler_params=pltpu.CompilerParams(vmem_limit_bytes=VMEM_MIB * 2**20),
        cost_estimate=pl.CostEstimate(flops=cost, bytes_accessed=cost, transcendentals=0),
        name=name,
    )(*args)


def swap(x, k):
    return lax.ppermute(x, "replica", [(i, i ^ k) for i in range(4)])


def swap_around(x):
    pairs = [(64 * i + f, 64 * (i ^ 3) + (f ^ 4)) for i in range(4) for f in range(64)]
    return lax.ppermute(x, ("replica", "fsdp"), pairs)


def prologue(r, local, momentum):
    def body(r_ref, l_ref, m_ref, half_ref, *refs):
        outs, (m, sems) = refs[:4], refs[4:]
        copies = Copies(sems)
        loads = [
            copies.start(m_ref.at[pl.ds(p * 512, 512), :], m.at[pl.ds(p * 512, 512), :])
            for p in range(4)
        ]
        other = 1 - r_ref[0] % 2
        copies.send(l_ref.at[at(other * 64, 64), :], half_ref)
        for p in range(4):
            loads[p].wait()
            for k in range(4):
                seg = seg_of(peer(r_ref[0], k))
                for j in range(4 * p, 4 * p + 4):
                    outs[k][j] = m[at(j * 128 + seg * 32, 32), :].astype(BF)
        copies.finish()

    return call(
        body, "prologue", SHORT, [shape(64, 8192)] + [shape(16, 32, 128)] * 4,
        [r, local, momentum], [shape(2048, 128, dtype=F32)], 5, out_near=True,
    )


def in_order(r, pieces, after):
    def body(r_ref, after_ref, *refs):
        for k in range(4):
            refs[4][peer(r_ref[0], k)] = refs[3 - k][...]

    return call(
        body, "in_order", LONG, shape(4, 16, 32, 128), [r, after, *pieces[::-1]], [], 1,
        near=2, out_near=True,
    )


def inner(step):
    lax.fori_loop(0, WIDTH // INNER, lambda i, c: (step(at(i * INNER, INNER)), c)[1], 0)


def partial_for_other(r, local, theirs, anchor, after):
    def body(r_ref, l_ref, t_ref, a_ref, after_ref, o_ref, l, t, a, o, sems):
        mine = at(seg_of(peer(r_ref[0], 2)) * 32, 32)
        half = at((1 - r_ref[0] // 2) * 32, 32)
        copies = Copies(sems)
        loads = []
        for p in range(PARTS):
            cols = pl.ds(p * WIDTH, WIDTH)
            loads.append([
                copies.start(l_ref.at[mine, cols], l.at[p]),
                copies.start(t_ref.at[half, cols], t.at[p]),
                copies.start(a_ref.at[mine, cols], a.at[p]),
            ])
        for p in range(PARTS):
            for load in loads[p]:
                load.wait()

            def step(cols, p=p):
                x = a[p, :, cols].astype(F32)
                total = (x - l[p, :, cols].astype(F32)) + (x - t[p, :, cols].astype(F32))
                o[p, :, cols] = total.astype(BF)

            inner(step)
            copies.send(o.at[p], o_ref.at[:, pl.ds(p * WIDTH, WIDTH)])
        copies.finish()

    return call(
        body, "partial_for_other", SHORT, shape(32, 8192), [r, local, theirs, anchor, after],
        [shape(PARTS, 32, WIDTH)] * 4, 4 * PARTS,
    )


def average_rows(r, local, theirs, anchor, partial):
    def body(r_ref, l_ref, t_ref, a_ref, p_ref, avg_ref, *refs):
        outs, (l, t, a, q, avg, cut, sems) = refs[:4], refs[4:]
        mine = at(seg_of(r_ref[0]) * 32, 32)
        half = at((r_ref[0] // 2) * 32, 32)
        copies = Copies(sems)
        loads = []
        for k in range(4):
            cols = at(peer(r_ref[0], k) * WIDTH, WIDTH)
            loads.append([
                copies.start(l_ref.at[mine, cols], l.at[k]),
                copies.start(t_ref.at[half, cols], t.at[k]),
                copies.start(a_ref.at[mine, cols], a.at[k]),
                copies.start(p_ref.at[:, cols], q.at[k]),
            ])
        for k in range(4):
            for load in loads[k]:
                load.wait()

            def step(i, carry, k=k):
                cols = at(i * INNER, INNER)
                x = a[k, :, cols].astype(F32)
                own = (x - l[k, :, cols].astype(F32)) + (x - t[k, :, cols].astype(F32))
                y = (own + q[k, :, cols].astype(F32)) * 0.25
                avg[k, :, cols] = y
                narrow = y.astype(BF)
                for n in range(INNER // 128):
                    cut[k, i * (INNER // 128) + n] = narrow[:, n * 128 : (n + 1) * 128]
                return carry

            lax.fori_loop(0, WIDTH // INNER, step, 0)
            copies.send(cut.at[k], outs[k])
            copies.send(avg.at[k], avg_ref.at[:, at(peer(r_ref[0], k) * WIDTH, WIDTH)])
        copies.finish()

    return call(
        body, "average_rows", LONG, [shape(32, 8192, dtype=F32)] + [shape(16, 32, 128)] * 4,
        [r, local, theirs, anchor, partial],
        [shape(4, 32, WIDTH)] * 4 + [shape(4, 32, WIDTH, dtype=F32), shape(4, 16, 32, 128)], 24,
    )


def stack_pieces(r, pieces):
    def body(r_ref, *refs):
        for k in range(4):
            refs[4][:, k] = refs[k][...]

    return call(
        body, "stack_pieces", SHORT, shape(16, 4, 32, 128), [r, *pieces], [], 1,
        near=1, out_near=True,
    )


def change_rows(rg, average, m_rows):
    def body(rg_ref, avg_ref, m_ref, o_ref, avg, m, o, sems):
        flip = jnp.where(peer(rg_ref[0], rg_ref[1]) == 3, 4, 0)
        copies = Copies(sems)
        loads = [
            (
                copies.start(avg_ref.at[:, pl.ds(p * WIDTH, WIDTH)], avg.at[p]),
                copies.start(m_ref.at[pl.ds(p * 16, 16)], m.at[p]),
            )
            for p in range(PARTS)
        ]
        for p in range(PARTS):
            for load in loads[p]:
                load.wait()

            def step(n, carry, p=p):
                cols = at(n * 128, 128)
                x = avg[p, :, cols]
                momentum = outer_beta * m[p, peer(n, flip)].astype(F32) + x
                o[p, :, cols] = (outer_rate * (x + outer_beta * momentum)).astype(BF)
                return carry

            lax.fori_loop(0, 16, step, 0, unroll=4)
            copies.send(o.at[p], o_ref.at[:, pl.ds(p * WIDTH, WIDTH)])
        copies.finish()

    return call(
        body, "change_rows", SHORT, shape(32, 8192), [rg, average, m_rows],
        [shape(PARTS, 32, WIDTH, dtype=F32), shape(4, 16, 32, 128), shape(PARTS, 32, WIDTH)],
        3 * PARTS,
    )


def new_momentum_of(rg, momentum, pieces, after):
    def body(rg_ref, after_ref, p_ref, m_ref, o_ref, q, o, sems):
        copies = Copies(sems)
        copies.send(p_ref, q)
        copies.finish()
        copies.open = []
        r, g = rg_ref[0], rg_ref[1]
        for p in range(4):
            for k in range(4):
                other = peer(g, k)
                flip = jnp.where(other // 2 == r // 2, 0, 4)
                for j in range(4):
                    rows = at(j * 128 + seg_of(other) * 32, 32)
                    all_rows = at((4 * p + j) * 128 + seg_of(other) * 32, 32)
                    piece = q[peer(4 * p + j, flip), k].astype(F32)
                    o[p, rows, :] = outer_beta * m_ref[all_rows, :] + piece
            copies.send(o.at[p], o_ref.at[pl.ds(p * 512, 512), :])
        copies.finish()

    return call(
        body, "new_momentum_of", SHORT, shape(2048, 128, dtype=F32),
        [rg, after, pieces, momentum], [shape(16, 4, 32, 128), shape(4, 512, 128, dtype=F32)], 5,
        near=3,
    )


def outputs_of(r, local, anchor, changes, before):
    ks = sorted(changes)
    n = len(ks)

    def body(r_ref, l_ref, a_ref, *refs):
        new_ref, mixed_ref, l, a, c, new, mixed, sems = refs[-8:]
        copies = Copies(sems)
        loads = []
        for m, k in enumerate(ks):
            rows = at(seg_of(peer(r_ref[0], k)) * 32, 32)
            for p in range(PARTS):
                cols = pl.ds(p * WIDTH, WIDTH)
                i = m * PARTS + p
                loads.append((
                    rows,
                    cols,
                    copies.start(l_ref.at[rows, cols], l.at[i]),
                    copies.start(a_ref.at[rows, cols], a.at[i]),
                    copies.start(refs[m].at[:, cols], c.at[i]),
                ))
        for i, (rows, cols, *waits) in enumerate(loads):
            for load in waits:
                load.wait()

            def step(x, i=i):
                global_new = a[i, :, x].astype(F32) - c[i, :, x].astype(F32)
                new[i, :, x] = global_new.astype(BF)
                mixed[i, :, x] = (
                    mix_weight * l[i, :, x].astype(F32) + (1.0 - mix_weight) * global_new
                ).astype(BF)

            inner(step)
            copies.send(new.at[i], new_ref.at[rows, cols])
            copies.send(mixed.at[i], mixed_ref.at[rows, cols])
        copies.finish()

    return call(
        body, "outputs_of", SHORT, [shape(128, 8192)] * 2,
        [r, local, anchor, *[changes[k] for k in ks], *before],
        [shape(n * PARTS, 32, WIDTH)] * 5, 5 * n * PARTS,
        {3 + n + b: b for b in range(len(before))},
    )


def across(x, k):
    pairs = [
        (64 * r + 16 * g + q, 64 * g + 16 * (r ^ k) + (q if r // 2 == g // 2 else q ^ 4))
        for r in range(4)
        for g in range(4)
        for q in range(16)
    ]
    return lax.ppermute(x, ("replica", "fsdp"), pairs)


def in_hbm(x):
    return pltpu.with_memory_space_constraint(x, pltpu.HBM)


def local(local_weights, anchor, momentum):
    own, anchor = in_hbm(local_weights[0]), in_hbm(anchor)
    r = lax.axis_index("replica")[None].astype(jnp.int32)
    g = (lax.axis_index("fsdp") // 16)[None].astype(jnp.int32)
    rg = jnp.concatenate([r, g])

    half, *pieces = prologue(r, own, in_hbm(momentum))
    theirs = swap(half, 1)
    pieces = [pieces[0], swap(pieces[1], 1), swap(pieces[2], 2), swap_around(pieces[3])]
    for_other = partial_for_other(r, own, theirs, anchor, pieces[0])
    partial = swap(for_other, 2)
    by_row = in_order(r, pieces, for_other).reshape(64, 32, 128)
    m_rows = lax.all_to_all(by_row, "fsdp", 0, 0, tiled=True)

    average, *cut = average_rows(r, own, theirs, anchor, in_hbm(partial))
    cut = stack_pieces(r, [across(x, k) for k, x in enumerate(cut)])
    groups = [[16 * i + q for q in range(16)] for i in range(4)]
    cut = lax.all_to_all(cut, "fsdp", 0, 0, axis_index_groups=groups, tiled=True)

    change = change_rows(rg, average, m_rows)
    change2 = swap(change, 2)
    change1 = swap(change, 1)
    change3 = swap(change2, 1)
    outs = outputs_of(r, own, anchor, {0: change, 1: change1}, ())
    outs = outputs_of(r, own, anchor, {2: change2}, outs)
    new_anchor, mixed = outputs_of(r, own, anchor, {3: change3}, outs)
    new_momentum = new_momentum_of(rg, momentum, cut, in_hbm(mixed))
    return new_momentum, new_anchor, mixed[None]


def solution(mesh):
    return jax.shard_map(
        local,
        mesh=mesh,
        in_specs=(P("replica", "fsdp", None), P("fsdp", None), P("replica", "fsdp")),
        out_specs=(P("replica", "fsdp"), P("fsdp", None), P("replica", "fsdp", None)),
        check_vma=False,
    )
```

```python
import jax
import jax.numpy as jnp
from jax import lax
from jax.experimental import pallas as pl
from jax.experimental.pallas import tpu as pltpu
from jax.sharding import PartitionSpec as P

outer_rate = 0.7
outer_beta = 0.9
mix_weight = 0.5

BF = jnp.bfloat16
F32 = jnp.float32
PARTS = 4
WIDTH = 8192 // PARTS
INNER = 512
SHORT = 2 << 20
LONG = 1 << 34
VMEM_MIB = 16


def seg_of(r):
    return 2 * (r % 2) + r // 2


def peer(r, k):
    return jnp.bitwise_xor(r, k)


def shape(*dims, dtype=BF):
    return jax.ShapeDtypeStruct(dims, dtype)


def at(start, count):
    return pl.ds(pl.multiple_of(start, count), count)


class Copies:
    def __init__(self, sems):
        self.sems, self.count, self.open = sems, 0, []

    def start(self, src, dst):
        copy = pltpu.make_async_copy(src, dst, self.sems.at[self.count])
        copy.start()
        self.count += 1
        return copy

    def send(self, src, dst):
        self.open.append(self.start(src, dst))

    def finish(self):
        for copy in self.open:
            copy.wait()


class Place:
    def __getitem__(self, i):
        return lax.axis_index("fsdp") // 16 if i else lax.axis_index("replica")


def call(body, name, cost, outs, args, scratch, copies, aliases=None, near=None, out_near=False):
    anywhere = pl.BlockSpec(memory_space=pl.ANY)
    whole = pl.BlockSpec(memory_space=pltpu.VMEM)
    near = len(args) if near is None else near
    out_spec = whole if out_near else anywhere
    single = not isinstance(outs, list)
    count = 1 if single else len(outs)
    return pl.pallas_call(
        lambda *refs: body(Place(), *refs),
        out_shape=outs,
        in_specs=[anywhere] * near + [whole] * (len(args) - near),
        out_specs=out_spec if single else [out_spec] * count,
        scratch_shapes=[pltpu.VMEM(x.shape, x.dtype) for x in scratch]
        + [pltpu.SemaphoreType.DMA((copies,))],
        input_output_aliases=aliases or {},
        compiler_params=pltpu.CompilerParams(vmem_limit_bytes=VMEM_MIB * 2**20),
        cost_estimate=pl.CostEstimate(flops=cost, bytes_accessed=cost, transcendentals=0),
        name=name,
    )(*args)


def swap(x, k):
    return lax.ppermute(x, "replica", [(i, i ^ k) for i in range(4)])


def swap_around(x):
    pairs = [(64 * i + f, 64 * (i ^ 3) + (f ^ 4)) for i in range(4) for f in range(64)]
    return lax.ppermute(x, ("replica", "fsdp"), pairs)


def prologue(local, momentum):
    def body(r_ref, l_ref, m_ref, half_ref, *refs):
        outs, (m, sems) = refs[:4], refs[4:]
        copies = Copies(sems)
        loads = [
            copies.start(m_ref.at[pl.ds(p * 512, 512), :], m.at[pl.ds(p * 512, 512), :])
            for p in range(4)
        ]
        other = 1 - r_ref[0] % 2
        copies.send(l_ref.at[at(other * 64, 64), :], half_ref)
        for p in range(4):
            loads[p].wait()
            for k in range(4):
                seg = seg_of(peer(r_ref[0], k))
                for j in range(4 * p, 4 * p + 4):
                    outs[k][j] = m[at(j * 128 + seg * 32, 32), :].astype(BF)
        copies.finish()

    return call(
        body, "prologue", SHORT, [shape(64, 8192)] + [shape(16, 32, 128)] * 4,
        [local, momentum], [shape(2048, 128, dtype=F32)], 5, out_near=True,
    )


def in_order(pieces, after):
    def body(r_ref, after_ref, *refs):
        for k in range(4):
            refs[4][peer(r_ref[0], k)] = refs[3 - k][...]

    return call(
        body, "in_order", LONG, shape(4, 16, 32, 128), [after, *pieces[::-1]], [], 1,
        near=1, out_near=True,
    )


def inner(step):
    lax.fori_loop(
        0, WIDTH // INNER, lambda i, c: (step(at(i * INNER, INNER)), c)[1], 0, unroll=True
    )


def partial_for_other(local, theirs, anchor, after):
    def body(r_ref, l_ref, t_ref, a_ref, after_ref, o_ref, l, t, a, o, sems):
        mine = at(seg_of(peer(r_ref[0], 2)) * 32, 32)
        half = at((1 - r_ref[0] // 2) * 32, 32)
        copies = Copies(sems)
        loads = []
        for p in range(PARTS):
            cols = pl.ds(p * WIDTH, WIDTH)
            loads.append([
                copies.start(l_ref.at[mine, cols], l.at[p]),
                copies.start(t_ref.at[half, cols], t.at[p]),
                copies.start(a_ref.at[mine, cols], a.at[p]),
            ])
        for p in range(PARTS):
            for load in loads[p]:
                load.wait()

            def step(cols, p=p):
                x = a[p, :, cols].astype(F32)
                total = (x - l[p, :, cols].astype(F32)) + (x - t[p, :, cols].astype(F32))
                o[p, :, cols] = total.astype(BF)

            inner(step)
            copies.send(o.at[p], o_ref.at[:, pl.ds(p * WIDTH, WIDTH)])
        copies.finish()

    return call(
        body, "partial_for_other", SHORT, shape(32, 8192), [local, theirs, anchor, after],
        [shape(PARTS, 32, WIDTH)] * 4, 4 * PARTS,
    )


def average_rows(local, theirs, anchor, partial):
    def body(r_ref, l_ref, t_ref, a_ref, p_ref, avg_ref, *refs):
        outs, (l, t, a, q, avg, cut, sems) = refs[:4], refs[4:]
        mine = at(seg_of(r_ref[0]) * 32, 32)
        half = at((r_ref[0] // 2) * 32, 32)
        copies = Copies(sems)
        loads = []
        for k in range(4):
            cols = at(peer(r_ref[0], k) * WIDTH, WIDTH)
            loads.append([
                copies.start(l_ref.at[mine, cols], l.at[k]),
                copies.start(t_ref.at[half, cols], t.at[k]),
                copies.start(a_ref.at[mine, cols], a.at[k]),
                copies.start(p_ref.at[:, cols], q.at[k]),
            ])
        for k in range(4):
            for load in loads[k]:
                load.wait()

            def step(i, carry, k=k):
                cols = at(i * INNER, INNER)
                x = a[k, :, cols].astype(F32)
                own = (x - l[k, :, cols].astype(F32)) + (x - t[k, :, cols].astype(F32))
                y = (own + q[k, :, cols].astype(F32)) * 0.25
                avg[k, :, cols] = y
                narrow = y.astype(BF)
                for n in range(INNER // 128):
                    cut[k, i * (INNER // 128) + n] = narrow[:, n * 128 : (n + 1) * 128]
                return carry

            lax.fori_loop(0, WIDTH // INNER, step, 0, unroll=True)
            copies.send(cut.at[k], outs[k])
            copies.send(avg.at[k], avg_ref.at[:, at(peer(r_ref[0], k) * WIDTH, WIDTH)])
        copies.finish()

    return call(
        body, "average_rows", LONG, [shape(32, 8192, dtype=F32)] + [shape(16, 32, 128)] * 4,
        [local, theirs, anchor, partial],
        [shape(4, 32, WIDTH)] * 4 + [shape(4, 32, WIDTH, dtype=F32), shape(4, 16, 32, 128)], 24,
    )


def stack_pieces(pieces):
    def body(r_ref, *refs):
        for k in range(4):
            refs[4][:, k] = refs[k][...]

    return call(
        body, "stack_pieces", SHORT, shape(16, 4, 32, 128), [*pieces], [], 1,
        near=0, out_near=True,
    )


def change_rows(average, m_rows):
    def body(rg_ref, avg_ref, m_ref, o_ref, avg, m, o, sems):
        flip = jnp.where(peer(rg_ref[0], rg_ref[1]) == 3, 4, 0)
        copies = Copies(sems)
        loads = [
            (
                copies.start(avg_ref.at[:, pl.ds(p * WIDTH, WIDTH)], avg.at[p]),
                copies.start(m_ref.at[pl.ds(p * 16, 16)], m.at[p]),
            )
            for p in range(PARTS)
        ]
        for p in range(PARTS):
            for load in loads[p]:
                load.wait()

            def step(n, carry, p=p):
                cols = at(n * 128, 128)
                x = avg[p, :, cols]
                momentum = outer_beta * m[p, peer(n, flip)].astype(F32) + x
                o[p, :, cols] = (outer_rate * (x + outer_beta * momentum)).astype(BF)
                return carry

            lax.fori_loop(0, 16, step, 0, unroll=4)
            copies.send(o.at[p], o_ref.at[:, pl.ds(p * WIDTH, WIDTH)])
        copies.finish()

    return call(
        body, "change_rows", SHORT, shape(32, 8192), [average, m_rows],
        [shape(PARTS, 32, WIDTH, dtype=F32), shape(4, 16, 32, 128), shape(PARTS, 32, WIDTH)],
        3 * PARTS,
    )


def new_momentum_of(momentum, pieces, after):
    def body(rg_ref, after_ref, p_ref, m_ref, o_ref, q, o, sems):
        copies = Copies(sems)
        copies.send(p_ref, q)
        copies.finish()
        copies.open = []
        r, g = rg_ref[0], rg_ref[1]
        for p in range(4):
            for k in range(4):
                other = peer(g, k)
                flip = jnp.where(other // 2 == r // 2, 0, 4)
                for j in range(4):
                    rows = at(j * 128 + seg_of(other) * 32, 32)
                    all_rows = at((4 * p + j) * 128 + seg_of(other) * 32, 32)
                    piece = q[peer(4 * p + j, flip), k].astype(F32)
                    o[p, rows, :] = outer_beta * m_ref[all_rows, :] + piece
            copies.send(o.at[p], o_ref.at[pl.ds(p * 512, 512), :])
        copies.finish()

    return call(
        body, "new_momentum_of", SHORT, shape(2048, 128, dtype=F32),
        [after, pieces, momentum], [shape(16, 4, 32, 128), shape(4, 512, 128, dtype=F32)], 5,
        near=2,
    )


def outputs_of(local, anchor, changes, before):
    ks = sorted(changes)
    n = len(ks)

    def body(r_ref, l_ref, a_ref, *refs):
        new_ref, mixed_ref, l, a, c, new, mixed, sems = refs[-8:]
        copies = Copies(sems)
        loads = []
        for m, k in enumerate(ks):
            rows = at(seg_of(peer(r_ref[0], k)) * 32, 32)
            for p in range(PARTS):
                cols = pl.ds(p * WIDTH, WIDTH)
                i = m * PARTS + p
                loads.append((
                    rows,
                    cols,
                    copies.start(l_ref.at[rows, cols], l.at[i]),
                    copies.start(a_ref.at[rows, cols], a.at[i]),
                    copies.start(refs[m].at[:, cols], c.at[i]),
                ))
        for i, (rows, cols, *waits) in enumerate(loads):
            for load in waits:
                load.wait()

            def step(x, i=i):
                global_new = a[i, :, x].astype(F32) - c[i, :, x].astype(F32)
                new[i, :, x] = global_new.astype(BF)
                mixed[i, :, x] = (
                    mix_weight * l[i, :, x].astype(F32) + (1.0 - mix_weight) * global_new
                ).astype(BF)

            inner(step)
            copies.send(new.at[i], new_ref.at[rows, cols])
            copies.send(mixed.at[i], mixed_ref.at[rows, cols])
        copies.finish()

    return call(
        body, "outputs_of", SHORT, [shape(128, 8192)] * 2,
        [local, anchor, *[changes[k] for k in ks], *before],
        [shape(n * PARTS, 32, WIDTH)] * 5, 5 * n * PARTS,
        {2 + n + b: b for b in range(len(before))},
    )


def across(x, k):
    pairs = [
        (64 * r + 16 * g + q, 64 * g + 16 * (r ^ k) + (q if r // 2 == g // 2 else q ^ 4))
        for r in range(4)
        for g in range(4)
        for q in range(16)
    ]
    return lax.ppermute(x, ("replica", "fsdp"), pairs)


def in_hbm(x):
    return pltpu.with_memory_space_constraint(x, pltpu.HBM)


def local(local_weights, anchor, momentum):
    own, anchor = in_hbm(local_weights[0]), in_hbm(anchor)

    half, *pieces = prologue(own, in_hbm(momentum))
    theirs = swap(half, 1)
    pieces = [pieces[0], swap(pieces[1], 1), swap(pieces[2], 2), swap_around(pieces[3])]
    for_other = partial_for_other(own, theirs, anchor, pieces[0])
    partial = swap(for_other, 2)
    by_row = in_order(pieces, for_other).reshape(64, 32, 128)
    m_rows = lax.all_to_all(by_row, "fsdp", 0, 0, tiled=True)

    average, *cut = average_rows(own, theirs, anchor, in_hbm(partial))
    cut = stack_pieces([across(x, k) for k, x in enumerate(cut)])
    groups = [[16 * i + q for q in range(16)] for i in range(4)]
    cut = lax.all_to_all(cut, "fsdp", 0, 0, axis_index_groups=groups, tiled=True)

    change = change_rows(average, m_rows)
    change2 = swap(change, 2)
    change1 = swap(change, 1)
    change3 = swap(change2, 1)
    outs = outputs_of(own, anchor, {0: change, 1: change1}, ())
    outs = outputs_of(own, anchor, {2: change2}, outs)
    new_anchor, mixed = outputs_of(own, anchor, {3: change3}, outs)
    new_momentum = new_momentum_of(momentum, cut, in_hbm(mixed))
    return new_momentum, new_anchor, mixed[None]


def solution(mesh):
    return jax.shard_map(
        local,
        mesh=mesh,
        in_specs=(P("replica", "fsdp", None), P("fsdp", None), P("replica", "fsdp")),
        out_specs=(P("replica", "fsdp"), P("fsdp", None), P("replica", "fsdp", None)),
        check_vma=False,
    )
```

```python
import jax
import jax.numpy as jnp
from jax import lax
from jax.experimental import pallas as pl
from jax.experimental.pallas import tpu as pltpu
from jax.sharding import PartitionSpec as P

outer_rate = 0.7
outer_beta = 0.9
mix_weight = 0.5

BF = jnp.bfloat16
F32 = jnp.float32
PARTS = 4
WIDTH = 8192 // PARTS
INNER = 512
SHORT = 2 << 20
LONG = 1 << 34
VMEM_MIB = 16


def seg_of(r):
    return 2 * (r % 2) + r // 2


def peer(r, k):
    return jnp.bitwise_xor(r, k)


def shape(*dims, dtype=BF):
    return jax.ShapeDtypeStruct(dims, dtype)


def at(start, count):
    return pl.ds(pl.multiple_of(start, count), count)


class Copies:
    def __init__(self, sems):
        self.sems, self.count, self.open = sems, 0, []

    def start(self, src, dst):
        copy = pltpu.make_async_copy(src, dst, self.sems.at[self.count])
        copy.start()
        self.count += 1
        return copy

    def send(self, src, dst):
        self.open.append(self.start(src, dst))

    def finish(self):
        for copy in self.open:
            copy.wait()


class Place:
    def __getitem__(self, i):
        return lax.axis_index("fsdp") // 16 if i else lax.axis_index("replica")


def call(body, name, cost, outs, args, scratch, copies, aliases=None, near=None, out_near=False):
    anywhere = pl.BlockSpec(memory_space=pl.ANY)
    whole = pl.BlockSpec(memory_space=pltpu.VMEM)
    near = len(args) if near is None else near
    out_spec = whole if out_near else anywhere
    single = not isinstance(outs, list)
    count = 1 if single else len(outs)
    return pl.pallas_call(
        lambda *refs: body(Place(), *refs),
        out_shape=outs,
        in_specs=[anywhere] * near + [whole] * (len(args) - near),
        out_specs=out_spec if single else [out_spec] * count,
        scratch_shapes=[pltpu.VMEM(x.shape, x.dtype) for x in scratch]
        + [pltpu.SemaphoreType.DMA((copies,))],
        input_output_aliases=aliases or {},
        compiler_params=pltpu.CompilerParams(vmem_limit_bytes=VMEM_MIB * 2**20),
        cost_estimate=pl.CostEstimate(flops=cost, bytes_accessed=cost, transcendentals=0),
        name=name,
    )(*args)


def swap(x, k):
    return lax.ppermute(x, "replica", [(i, i ^ k) for i in range(4)])


def swap_around(x):
    pairs = [(64 * i + f, 64 * (i ^ 3) + (f ^ 4)) for i in range(4) for f in range(64)]
    return lax.ppermute(x, ("replica", "fsdp"), pairs)


def prologue(local, momentum):
    def body(r_ref, l_ref, m_ref, half_ref, *refs):
        outs, (m, sems) = refs[:4], refs[4:]
        copies = Copies(sems)
        loads = [
            copies.start(m_ref.at[pl.ds(p * 512, 512), :], m.at[pl.ds(p * 512, 512), :])
            for p in range(4)
        ]
        other = 1 - r_ref[0] % 2
        copies.send(l_ref.at[at(other * 64, 64), :], half_ref)
        for p in range(4):
            loads[p].wait()
            for k in range(4):
                seg = seg_of(peer(r_ref[0], k))
                for j in range(4 * p, 4 * p + 4):
                    outs[k][j] = m[at(j * 128 + seg * 32, 32), :].astype(BF)
        copies.finish()

    return call(
        body, "prologue", SHORT, [shape(64, 8192)] + [shape(16, 32, 128)] * 4,
        [local, momentum], [shape(2048, 128, dtype=F32)], 5, out_near=True,
    )


def in_order(pieces, after):
    def body(r_ref, after_ref, *refs):
        for k in range(4):
            refs[4][peer(r_ref[0], k)] = refs[3 - k][...]

    return call(
        body, "in_order", LONG, shape(4, 16, 32, 128), [after, *pieces[::-1]], [], 1,
        near=1, out_near=True,
    )


def inner(step):
    lax.fori_loop(
        0, WIDTH // INNER, lambda i, c: (step(at(i * INNER, INNER)), c)[1], 0, unroll=True
    )


def partial_rows(local, theirs, anchor):
    def body(r_ref, l_ref, t_ref, a_ref, other_ref, own_ref, l, t, a, o, own, sems):
        copies = Copies(sems)
        loads = []
        for k in (2, 0):
            device = peer(r_ref[0], k)
            mine = at(seg_of(device) * 32, 32)
            half = at((device // 2) * 32, 32)
            for p in range(PARTS):
                cols = pl.ds(p * WIDTH, WIDTH)
                i = len(loads)
                loads.append([
                    copies.start(l_ref.at[mine, cols], l.at[i]),
                    copies.start(t_ref.at[half, cols], t.at[i]),
                    copies.start(a_ref.at[mine, cols], a.at[i]),
                ])
        for i, waits in enumerate(loads):
            for load in waits:
                load.wait()
            to, p = (o if i < PARTS else own), i % PARTS

            def step(cols, i=i, p=p, to=to):
                x = a[i, :, cols].astype(F32)
                total = (x - l[i, :, cols].astype(F32)) + (x - t[i, :, cols].astype(F32))
                to[p, :, cols] = total.astype(to.dtype)

            inner(step)
            to_ref = other_ref if i < PARTS else own_ref
            copies.send(to.at[p], to_ref.at[:, pl.ds(p * WIDTH, WIDTH)])
        copies.finish()

    return call(
        body, "partial_rows", SHORT, [shape(32, 8192)] * 2,
        [local, theirs, anchor],
        [shape(2 * PARTS, 32, WIDTH)] * 3
        + [shape(PARTS, 32, WIDTH)] * 2,
        8 * PARTS,
    )


def average_rows(own, partial):
    def body(r_ref, own_ref, p_ref, avg_ref, *refs):
        outs, (x, q, avg, cut, sems) = refs[:4], refs[4:]
        copies = Copies(sems)
        loads = []
        for k in range(4):
            cols = at(peer(r_ref[0], k) * WIDTH, WIDTH)
            loads.append([
                copies.start(own_ref.at[:, cols], x.at[k]),
                copies.start(p_ref.at[:, cols], q.at[k]),
            ])
        for k in range(4):
            for load in loads[k]:
                load.wait()

            def step(i, carry, k=k):
                cols = at(i * INNER, INNER)
                y = (x[k, :, cols].astype(F32) + q[k, :, cols].astype(F32)) * 0.25
                avg[k, :, cols] = y
                narrow = y.astype(BF)
                for n in range(INNER // 128):
                    cut[k, i * (INNER // 128) + n] = narrow[:, n * 128 : (n + 1) * 128]
                return carry

            lax.fori_loop(0, WIDTH // INNER, step, 0, unroll=True)
            copies.send(cut.at[k], outs[k])
            copies.send(avg.at[k], avg_ref.at[:, at(peer(r_ref[0], k) * WIDTH, WIDTH)])
        copies.finish()

    return call(
        body, "average_rows", LONG, [shape(32, 8192, dtype=F32)] + [shape(16, 32, 128)] * 4,
        [own, partial],
        [shape(4, 32, WIDTH)] * 2 + [shape(4, 32, WIDTH, dtype=F32), shape(4, 16, 32, 128)], 16,
    )


def stack_pieces(pieces):
    def body(r_ref, *refs):
        for k in range(4):
            refs[4][:, k] = refs[k][...]

    return call(
        body, "stack_pieces", SHORT, shape(16, 4, 32, 128), [*pieces], [], 1,
        near=0, out_near=True,
    )


def change_rows(average, m_rows):
    def body(rg_ref, avg_ref, m_ref, o_ref, avg, m, o, sems):
        flip = jnp.where(peer(rg_ref[0], rg_ref[1]) == 3, 4, 0)
        copies = Copies(sems)
        loads = [
            (
                copies.start(avg_ref.at[:, pl.ds(p * WIDTH, WIDTH)], avg.at[p]),
                copies.start(m_ref.at[pl.ds(p * 16, 16)], m.at[p]),
            )
            for p in range(PARTS)
        ]
        for p in range(PARTS):
            for load in loads[p]:
                load.wait()

            def step(n, carry, p=p):
                cols = at(n * 128, 128)
                x = avg[p, :, cols]
                momentum = outer_beta * m[p, peer(n, flip)].astype(F32) + x
                o[p, :, cols] = (outer_rate * (x + outer_beta * momentum)).astype(BF)
                return carry

            lax.fori_loop(0, 16, step, 0, unroll=4)
            copies.send(o.at[p], o_ref.at[:, pl.ds(p * WIDTH, WIDTH)])
        copies.finish()

    return call(
        body, "change_rows", SHORT, shape(32, 8192), [average, m_rows],
        [shape(PARTS, 32, WIDTH, dtype=F32), shape(4, 16, 32, 128), shape(PARTS, 32, WIDTH)],
        3 * PARTS,
    )


def new_momentum_of(momentum, pieces, after):
    def body(rg_ref, after_ref, p_ref, m_ref, o_ref, q, o, sems):
        copies = Copies(sems)
        copies.send(p_ref, q)
        copies.finish()
        copies.open = []
        r, g = rg_ref[0], rg_ref[1]
        for p in range(4):
            for k in range(4):
                other = peer(g, k)
                flip = jnp.where(other // 2 == r // 2, 0, 4)
                for j in range(4):
                    rows = at(j * 128 + seg_of(other) * 32, 32)
                    all_rows = at((4 * p + j) * 128 + seg_of(other) * 32, 32)
                    piece = q[peer(4 * p + j, flip), k].astype(F32)
                    o[p, rows, :] = outer_beta * m_ref[all_rows, :] + piece
            copies.send(o.at[p], o_ref.at[pl.ds(p * 512, 512), :])
        copies.finish()

    return call(
        body, "new_momentum_of", SHORT, shape(2048, 128, dtype=F32),
        [after, pieces, momentum], [shape(16, 4, 32, 128), shape(4, 512, 128, dtype=F32)], 5,
        near=2,
    )


def outputs_of(local, anchor, changes, before):
    ks = sorted(changes)
    n = len(ks)

    def body(r_ref, l_ref, a_ref, *refs):
        new_ref, mixed_ref, l, a, c, new, mixed, sems = refs[-8:]
        copies = Copies(sems)
        loads = []
        for m, k in enumerate(ks):
            rows = at(seg_of(peer(r_ref[0], k)) * 32, 32)
            for p in range(PARTS):
                cols = pl.ds(p * WIDTH, WIDTH)
                i = m * PARTS + p
                loads.append((
                    rows,
                    cols,
                    copies.start(l_ref.at[rows, cols], l.at[i]),
                    copies.start(a_ref.at[rows, cols], a.at[i]),
                    copies.start(refs[m].at[:, cols], c.at[i]),
                ))
        for i, (rows, cols, *waits) in enumerate(loads):
            for load in waits:
                load.wait()

            def step(x, i=i):
                global_new = a[i, :, x].astype(F32) - c[i, :, x].astype(F32)
                new[i, :, x] = global_new.astype(BF)
                mixed[i, :, x] = (
                    mix_weight * l[i, :, x].astype(F32) + (1.0 - mix_weight) * global_new
                ).astype(BF)

            inner(step)
            copies.send(new.at[i], new_ref.at[rows, cols])
            copies.send(mixed.at[i], mixed_ref.at[rows, cols])
        copies.finish()

    return call(
        body, "outputs_of", SHORT, [shape(128, 8192)] * 2,
        [local, anchor, *[changes[k] for k in ks], *before],
        [shape(n * PARTS, 32, WIDTH)] * 5, 5 * n * PARTS,
        {2 + n + b: b for b in range(len(before))},
    )


def across(x, k):
    pairs = [
        (64 * r + 16 * g + q, 64 * g + 16 * (r ^ k) + (q if r // 2 == g // 2 else q ^ 4))
        for r in range(4)
        for g in range(4)
        for q in range(16)
    ]
    return lax.ppermute(x, ("replica", "fsdp"), pairs)


def in_hbm(x):
    return pltpu.with_memory_space_constraint(x, pltpu.HBM)


def local(local_weights, anchor, momentum):
    own, anchor = in_hbm(local_weights[0]), in_hbm(anchor)

    half, *pieces = prologue(own, in_hbm(momentum))
    theirs = swap(half, 1)
    pieces = [pieces[0], swap(pieces[1], 1), swap(pieces[2], 2), swap_around(pieces[3])]
    for_other, mine = partial_rows(own, theirs, anchor)
    partial = swap(for_other, 2)
    by_row = in_order(pieces, for_other).reshape(64, 32, 128)
    m_rows = lax.all_to_all(by_row, "fsdp", 0, 0, tiled=True)

    average, *cut = average_rows(mine, partial)
    cut = stack_pieces([across(x, k) for k, x in enumerate(cut)])
    groups = [[16 * i + q for q in range(16)] for i in range(4)]
    cut = lax.all_to_all(cut, "fsdp", 0, 0, axis_index_groups=groups, tiled=True)

    change = change_rows(average, m_rows)
    change2 = swap(change, 2)
    change1 = swap(change, 1)
    change3 = swap(change2, 1)
    outs = outputs_of(own, anchor, {0: change, 1: change1}, ())
    outs = outputs_of(own, anchor, {2: change2}, outs)
    new_anchor, mixed = outputs_of(own, anchor, {3: change3}, outs)
    new_momentum = new_momentum_of(momentum, cut, in_hbm(mixed))
    return new_momentum, new_anchor, mixed[None]


def solution(mesh):
    return jax.shard_map(
        local,
        mesh=mesh,
        in_specs=(P("replica", "fsdp", None), P("fsdp", None), P("replica", "fsdp")),
        out_specs=(P("replica", "fsdp"), P("fsdp", None), P("replica", "fsdp", None)),
        check_vma=False,
    )
```

```python
import jax
import jax.numpy as jnp
from jax import lax
from jax.experimental import pallas as pl
from jax.experimental.pallas import tpu as pltpu
from jax.sharding import PartitionSpec as P

outer_rate = 0.7
outer_beta = 0.9
mix_weight = 0.5

BF = jnp.bfloat16
F32 = jnp.float32
PARTS = 4
WIDTH = 8192 // PARTS
INNER = 512
SHORT = 2 << 20
LONG = 1 << 34
VMEM_MIB = 16


def seg_of(r):
    return 2 * (r % 2) + r // 2


def peer(r, k):
    return jnp.bitwise_xor(r, k)


def shape(*dims, dtype=BF):
    return jax.ShapeDtypeStruct(dims, dtype)


def at(start, count):
    return pl.ds(pl.multiple_of(start, count), count)


class Copies:
    def __init__(self, sems):
        self.sems, self.count, self.open = sems, 0, []

    def start(self, src, dst):
        copy = pltpu.make_async_copy(src, dst, self.sems.at[self.count])
        copy.start()
        self.count += 1
        return copy

    def send(self, src, dst):
        self.open.append(self.start(src, dst))

    def finish(self):
        for copy in self.open:
            copy.wait()


class Place:
    def __getitem__(self, i):
        return lax.axis_index("fsdp") // 16 if i else lax.axis_index("replica")


def call(body, name, cost, outs, args, scratch, copies, aliases=None, near=None, out_near=False,
         far=0):
    anywhere = pl.BlockSpec(memory_space=pl.ANY)
    whole = pl.BlockSpec(memory_space=pltpu.VMEM)
    near = len(args) if near is None else near
    out_spec = whole if out_near else anywhere
    single = not isinstance(outs, list)
    count = 1 if single else len(outs)
    return pl.pallas_call(
        lambda *refs: body(Place(), *refs),
        out_shape=outs,
        in_specs=[anywhere] * near + [whole] * (len(args) - near),
        out_specs=out_spec if single else [anywhere] * far + [out_spec] * (count - far),
        scratch_shapes=[pltpu.VMEM(x.shape, x.dtype) for x in scratch]
        + [pltpu.SemaphoreType.DMA((copies,))],
        input_output_aliases=aliases or {},
        compiler_params=pltpu.CompilerParams(vmem_limit_bytes=VMEM_MIB * 2**20),
        cost_estimate=pl.CostEstimate(flops=cost, bytes_accessed=cost, transcendentals=0),
        name=name,
    )(*args)


def swap(x, k):
    return lax.ppermute(x, "replica", [(i, i ^ k) for i in range(4)])


def swap_around(x):
    pairs = [(64 * i + f, 64 * (i ^ 3) + (f ^ 4)) for i in range(4) for f in range(64)]
    return lax.ppermute(x, ("replica", "fsdp"), pairs)


def prologue(local, momentum):
    def body(r_ref, l_ref, m_ref, half_ref, *refs):
        outs, (m, sems) = refs[:4], refs[4:]
        copies = Copies(sems)
        loads = [
            copies.start(m_ref.at[pl.ds(p * 512, 512), :], m.at[pl.ds(p * 512, 512), :])
            for p in range(4)
        ]
        other = 1 - r_ref[0] % 2
        copies.send(l_ref.at[at(other * 64, 64), :], half_ref)
        for p in range(4):
            loads[p].wait()
            for k in range(4):
                seg = seg_of(peer(r_ref[0], k))
                for j in range(4 * p, 4 * p + 4):
                    outs[k][j] = m[at(j * 128 + seg * 32, 32), :].astype(BF)
        copies.finish()

    return call(
        body, "prologue", SHORT, [shape(64, 8192)] + [shape(16, 32, 128)] * 4,
        [local, momentum], [shape(2048, 128, dtype=F32)], 5, out_near=True,
    )


def in_order(pieces, after):
    def body(r_ref, after_ref, *refs):
        for k in range(4):
            refs[4][peer(r_ref[0], k)] = refs[3 - k][...]

    return call(
        body, "in_order", LONG, shape(4, 16, 32, 128), [after, *pieces[::-1]], [], 1,
        near=1, out_near=True,
    )


def inner(step):
    lax.fori_loop(
        0, WIDTH // INNER, lambda i, c: (step(at(i * INNER, INNER)), c)[1], 0, unroll=True
    )


def partial_rows(local, theirs, anchor):
    def body(r_ref, l_ref, t_ref, a_ref, other_ref, own_ref, l, t, a, o, own, sems):
        copies = Copies(sems)
        loads = []
        for k in (2, 0):
            device = peer(r_ref[0], k)
            mine = at(seg_of(device) * 32, 32)
            half = at((device // 2) * 32, 32)
            for p in range(PARTS):
                cols = pl.ds(p * WIDTH, WIDTH)
                i = len(loads)
                loads.append([
                    copies.start(l_ref.at[mine, cols], l.at[i]),
                    copies.start(t_ref.at[half, cols], t.at[i]),
                    copies.start(a_ref.at[mine, cols], a.at[i]),
                ])
        for i, waits in enumerate(loads):
            for load in waits:
                load.wait()
            to, p = (o if i < PARTS else own), i % PARTS

            def step(cols, i=i, p=p, to=to):
                x = a[i, :, cols].astype(F32)
                total = (x - l[i, :, cols].astype(F32)) + (x - t[i, :, cols].astype(F32))
                to[p, :, cols] = total.astype(to.dtype)

            inner(step)
            to_ref = other_ref if i < PARTS else own_ref
            copies.send(to.at[p], to_ref.at[:, pl.ds(p * WIDTH, WIDTH)])
        copies.finish()

    return call(
        body, "partial_rows", SHORT, [shape(32, 8192)] * 2,
        [local, theirs, anchor],
        [shape(2 * PARTS, 32, WIDTH)] * 3
        + [shape(PARTS, 32, WIDTH)] * 2,
        8 * PARTS,
    )


def average_rows(own, partial):
    def body(r_ref, own_ref, p_ref, avg_ref, *refs):
        outs, (x, q, avg, sems) = refs[:4], refs[4:]
        copies = Copies(sems)
        loads = []
        for k in range(4):
            cols = at(peer(r_ref[0], k) * WIDTH, WIDTH)
            loads.append([
                copies.start(own_ref.at[:, cols], x.at[k]),
                copies.start(p_ref.at[:, cols], q.at[k]),
            ])
        for k in range(4):
            for load in loads[k]:
                load.wait()

            def step(i, carry, k=k):
                cols = at(i * INNER, INNER)
                y = (x[k, :, cols].astype(F32) + q[k, :, cols].astype(F32)) * 0.25
                avg[k, :, cols] = y
                narrow = y.astype(BF)
                for n in range(INNER // 128):
                    outs[k][i * (INNER // 128) + n] = narrow[:, n * 128 : (n + 1) * 128]
                return carry

            lax.fori_loop(0, WIDTH // INNER, step, 0, unroll=True)
            copies.send(avg.at[k], avg_ref.at[:, at(peer(r_ref[0], k) * WIDTH, WIDTH)])
        copies.finish()

    return call(
        body, "average_rows", LONG, [shape(32, 8192, dtype=F32)] + [shape(16, 32, 128)] * 4,
        [own, partial],
        [shape(4, 32, WIDTH)] * 2 + [shape(4, 32, WIDTH, dtype=F32)], 12, out_near=True, far=1,
    )


def stack_pieces(pieces):
    def body(r_ref, *refs):
        for k in range(4):
            refs[4][:, k] = refs[3 - k][...]

    return call(
        body, "stack_pieces", SHORT, shape(16, 4, 32, 128), pieces[::-1], [], 1,
        near=0, out_near=True,
    )


def change_rows(average, m_rows):
    def body(rg_ref, avg_ref, m_ref, o_ref, avg, m, o, sems):
        flip = jnp.where(peer(rg_ref[0], rg_ref[1]) == 3, 4, 0)
        copies = Copies(sems)
        loads = [
            (
                copies.start(avg_ref.at[:, pl.ds(p * WIDTH, WIDTH)], avg.at[p]),
                copies.start(m_ref.at[pl.ds(p * 16, 16)], m.at[p]),
            )
            for p in range(PARTS)
        ]
        for p in range(PARTS):
            for load in loads[p]:
                load.wait()

            def step(n, carry, p=p):
                cols = at(n * 128, 128)
                x = avg[p, :, cols]
                momentum = outer_beta * m[p, peer(n, flip)].astype(F32) + x
                o[p, :, cols] = (outer_rate * (x + outer_beta * momentum)).astype(BF)
                return carry

            lax.fori_loop(0, 16, step, 0, unroll=4)
            copies.send(o.at[p], o_ref.at[:, pl.ds(p * WIDTH, WIDTH)])
        copies.finish()

    return call(
        body, "change_rows", SHORT, shape(32, 8192), [average, m_rows],
        [shape(PARTS, 32, WIDTH, dtype=F32), shape(4, 16, 32, 128), shape(PARTS, 32, WIDTH)],
        3 * PARTS,
    )


def new_momentum_of(momentum, pieces, after):
    def body(rg_ref, after_ref, p_ref, m_ref, o_ref, q, o, sems):
        copies = Copies(sems)
        copies.send(p_ref, q)
        copies.finish()
        copies.open = []
        r, g = rg_ref[0], rg_ref[1]
        for p in range(4):
            for k in range(4):
                other = peer(g, k)
                flip = jnp.where(other // 2 == r // 2, 0, 4)
                for j in range(4):
                    rows = at(j * 128 + seg_of(other) * 32, 32)
                    all_rows = at((4 * p + j) * 128 + seg_of(other) * 32, 32)
                    piece = q[peer(4 * p + j, flip), k].astype(F32)
                    o[p, rows, :] = outer_beta * m_ref[all_rows, :] + piece
            copies.send(o.at[p], o_ref.at[pl.ds(p * 512, 512), :])
        copies.finish()

    return call(
        body, "new_momentum_of", SHORT, shape(2048, 128, dtype=F32),
        [after, pieces, momentum], [shape(16, 4, 32, 128), shape(4, 512, 128, dtype=F32)], 5,
        near=2,
    )


def outputs_of(local, anchor, changes, before):
    ks = sorted(changes)
    n = len(ks)

    def body(r_ref, l_ref, a_ref, *refs):
        new_ref, mixed_ref, l, a, c, new, mixed, sems = refs[-8:]
        copies = Copies(sems)
        loads = []
        for m, k in enumerate(ks):
            rows = at(seg_of(peer(r_ref[0], k)) * 32, 32)
            for p in range(PARTS):
                cols = pl.ds(p * WIDTH, WIDTH)
                i = m * PARTS + p
                loads.append((
                    rows,
                    cols,
                    copies.start(l_ref.at[rows, cols], l.at[i]),
                    copies.start(a_ref.at[rows, cols], a.at[i]),
                    copies.start(refs[m].at[:, cols], c.at[i]),
                ))
        for i, (rows, cols, *waits) in enumerate(loads):
            for load in waits:
                load.wait()

            def step(x, i=i):
                global_new = a[i, :, x].astype(F32) - c[i, :, x].astype(F32)
                new[i, :, x] = global_new.astype(BF)
                mixed[i, :, x] = (
                    mix_weight * l[i, :, x].astype(F32) + (1.0 - mix_weight) * global_new
                ).astype(BF)

            inner(step)
            copies.send(new.at[i], new_ref.at[rows, cols])
            copies.send(mixed.at[i], mixed_ref.at[rows, cols])
        copies.finish()

    return call(
        body, "outputs_of", SHORT, [shape(128, 8192)] * 2,
        [local, anchor, *[changes[k] for k in ks], *before],
        [shape(n * PARTS, 32, WIDTH)] * 5, 5 * n * PARTS,
        {2 + n + b: b for b in range(len(before))},
    )


def across(x, k):
    pairs = [
        (64 * r + 16 * g + q, 64 * g + 16 * (r ^ k) + (q if r // 2 == g // 2 else q ^ 4))
        for r in range(4)
        for g in range(4)
        for q in range(16)
    ]
    return lax.ppermute(x, ("replica", "fsdp"), pairs)


def in_hbm(x):
    return pltpu.with_memory_space_constraint(x, pltpu.HBM)


def local(local_weights, anchor, momentum):
    own, anchor = in_hbm(local_weights[0]), in_hbm(anchor)

    half, *pieces = prologue(own, in_hbm(momentum))
    theirs = swap(half, 1)
    pieces = [pieces[0], swap(pieces[1], 1), swap(pieces[2], 2), swap_around(pieces[3])]
    for_other, mine = partial_rows(own, theirs, anchor)
    partial = swap(for_other, 2)
    by_row = in_order(pieces, for_other).reshape(64, 32, 128)
    m_rows = lax.all_to_all(by_row, "fsdp", 0, 0, tiled=True)

    average, *cut = average_rows(mine, partial)
    cut = stack_pieces([across(x, k) for k, x in enumerate(cut)])
    groups = [[16 * i + q for q in range(16)] for i in range(4)]
    cut = lax.all_to_all(cut, "fsdp", 0, 0, axis_index_groups=groups, tiled=True)

    change = change_rows(average, m_rows)
    change2 = swap(change, 2)
    change1 = swap(change, 1)
    change3 = swap(change2, 1)
    outs = outputs_of(own, anchor, {0: change, 1: change1}, ())
    outs = outputs_of(own, anchor, {2: change2}, outs)
    new_anchor, mixed = outputs_of(own, anchor, {3: change3}, outs)
    new_momentum = new_momentum_of(momentum, cut, in_hbm(mixed))
    return new_momentum, new_anchor, mixed[None]


def solution(mesh):
    return jax.shard_map(
        local,
        mesh=mesh,
        in_specs=(P("replica", "fsdp", None), P("fsdp", None), P("replica", "fsdp")),
        out_specs=(P("replica", "fsdp"), P("fsdp", None), P("replica", "fsdp", None)),
        check_vma=False,
    )
```

```python
import jax
import jax.numpy as jnp
from jax import lax
from jax.experimental import pallas as pl
from jax.experimental.pallas import tpu as pltpu
from jax.sharding import PartitionSpec as P

outer_rate = 0.7
outer_beta = 0.9
mix_weight = 0.5

BF = jnp.bfloat16
F32 = jnp.float32
PARTS = 4
WIDTH = 8192 // PARTS
INNER = 512
SHORT = 2 << 20
LONG = 1 << 34
VMEM_MIB = 16


def seg_of(r):
    return 2 * (r % 2) + r // 2


def peer(r, k):
    return jnp.bitwise_xor(r, k)


def shape(*dims, dtype=BF):
    return jax.ShapeDtypeStruct(dims, dtype)


def at(start, count):
    return pl.ds(pl.multiple_of(start, count), count)


class Copies:
    def __init__(self, sems):
        self.sems, self.count, self.open = sems, 0, []

    def start(self, src, dst):
        copy = pltpu.make_async_copy(src, dst, self.sems.at[self.count])
        copy.start()
        self.count += 1
        return copy

    def send(self, src, dst):
        self.open.append(self.start(src, dst))

    def finish(self):
        for copy in self.open:
            copy.wait()


class Place:
    def __getitem__(self, i):
        return lax.axis_index("fsdp") // 16 if i else lax.axis_index("replica")


def call(body, name, cost, outs, args, scratch, copies, aliases=None, near=None, out_near=False,
         far=0):
    anywhere = pl.BlockSpec(memory_space=pl.ANY)
    whole = pl.BlockSpec(memory_space=pltpu.VMEM)
    near = len(args) if near is None else near
    out_spec = whole if out_near else anywhere
    single = not isinstance(outs, list)
    count = 1 if single else len(outs)
    return pl.pallas_call(
        lambda *refs: body(Place(), *refs),
        out_shape=outs,
        in_specs=[anywhere] * near + [whole] * (len(args) - near),
        out_specs=out_spec if single else [anywhere] * far + [out_spec] * (count - far),
        scratch_shapes=[pltpu.VMEM(x.shape, x.dtype) for x in scratch]
        + [pltpu.SemaphoreType.DMA((copies,))],
        input_output_aliases=aliases or {},
        compiler_params=pltpu.CompilerParams(vmem_limit_bytes=VMEM_MIB * 2**20),
        cost_estimate=pl.CostEstimate(flops=cost, bytes_accessed=cost, transcendentals=0),
        name=name,
    )(*args)


def swap(x, k):
    return lax.ppermute(x, "replica", [(i, i ^ k) for i in range(4)])


def swap_around(x):
    pairs = [(64 * i + f, 64 * (i ^ 3) + (f ^ 4)) for i in range(4) for f in range(64)]
    return lax.ppermute(x, ("replica", "fsdp"), pairs)


def prologue(local, momentum):
    def body(r_ref, l_ref, m_ref, half_ref, *refs):
        outs, (m, sems) = refs[:4], refs[4:]
        copies = Copies(sems)
        loads = [
            copies.start(m_ref.at[pl.ds(p * 512, 512), :], m.at[pl.ds(p * 512, 512), :])
            for p in range(4)
        ]
        other = 1 - r_ref[0] % 2
        copies.send(l_ref.at[at(other * 64, 64), :], half_ref)
        for p in range(4):
            loads[p].wait()
            for k in range(4):
                seg = seg_of(peer(r_ref[0], k))
                for j in range(4 * p, 4 * p + 4):
                    outs[k][j] = m[at(j * 128 + seg * 32, 32), :].astype(BF)
        copies.finish()

    return call(
        body, "prologue", SHORT, [shape(64, 8192)] + [shape(16, 32, 128)] * 4,
        [local, momentum], [shape(2048, 128, dtype=F32)], 5, out_near=True,
    )


def in_order(pieces, after):
    def body(r_ref, after_ref, *refs):
        for k in range(4):
            refs[4][peer(r_ref[0], k)] = refs[3 - k][...]

    return call(
        body, "in_order", LONG, shape(4, 16, 32, 128), [after, *pieces[::-1]], [], 1,
        near=1, out_near=True,
    )


def inner(step):
    lax.fori_loop(
        0, WIDTH // INNER, lambda i, c: (step(at(i * INNER, INNER)), c)[1], 0, unroll=True
    )


def partial_rows(local, theirs, anchor):
    def body(r_ref, l_ref, t_ref, a_ref, own_ref, other_ref, l, t, a, own, sems):
        copies = Copies(sems)
        loads = []
        for k in (2, 0):
            device = peer(r_ref[0], k)
            mine = at(seg_of(device) * 32, 32)
            half = at((device // 2) * 32, 32)
            for p in range(PARTS):
                cols = pl.ds(p * WIDTH, WIDTH)
                i = len(loads)
                loads.append([
                    copies.start(l_ref.at[mine, cols], l.at[i]),
                    copies.start(t_ref.at[half, cols], t.at[i]),
                    copies.start(a_ref.at[mine, cols], a.at[i]),
                ])
        for i, waits in enumerate(loads):
            for load in waits:
                load.wait()
            p = i % PARTS

            def step(n, carry, i=i, p=p):
                cols = at(n * INNER, INNER)
                x = a[i, :, cols].astype(F32)
                total = (x - l[i, :, cols].astype(F32)) + (x - t[i, :, cols].astype(F32))
                if i < PARTS:
                    other_ref[:, at(p * WIDTH + n * INNER, INNER)] = total.astype(BF)
                else:
                    own[p, :, cols] = total.astype(BF)
                return carry

            lax.fori_loop(0, WIDTH // INNER, step, 0, unroll=True)
            if i >= PARTS:
                copies.send(own.at[p], own_ref.at[:, pl.ds(p * WIDTH, WIDTH)])
        copies.finish()

    return call(
        body, "partial_rows", SHORT, [shape(32, 8192)] * 2,
        [local, theirs, anchor],
        [shape(2 * PARTS, 32, WIDTH)] * 3
        + [shape(PARTS, 32, WIDTH)],
        7 * PARTS, out_near=True, far=1,
    )


def average_rows(own, partial):
    def body(r_ref, own_ref, p_ref, avg_ref, *refs):
        outs, (x, q, avg, sems) = refs[:4], refs[4:]
        copies = Copies(sems)
        loads = []
        for k in range(4):
            cols = at(peer(r_ref[0], k) * WIDTH, WIDTH)
            loads.append([
                copies.start(own_ref.at[:, cols], x.at[k]),
                copies.start(p_ref.at[:, cols], q.at[k]),
            ])
        for k in range(4):
            for load in loads[k]:
                load.wait()

            def step(i, carry, k=k):
                cols = at(i * INNER, INNER)
                y = (x[k, :, cols].astype(F32) + q[k, :, cols].astype(F32)) * 0.25
                avg[k, :, cols] = y
                narrow = y.astype(BF)
                for n in range(INNER // 128):
                    outs[k][i * (INNER // 128) + n] = narrow[:, n * 128 : (n + 1) * 128]
                return carry

            lax.fori_loop(0, WIDTH // INNER, step, 0, unroll=True)
            copies.send(avg.at[k], avg_ref.at[:, at(peer(r_ref[0], k) * WIDTH, WIDTH)])
        copies.finish()

    return call(
        body, "average_rows", LONG, [shape(32, 8192, dtype=F32)] + [shape(16, 32, 128)] * 4,
        [own, partial],
        [shape(4, 32, WIDTH)] * 2 + [shape(4, 32, WIDTH, dtype=F32)], 12, out_near=True, far=1,
    )


def stack_pieces(pieces):
    def body(r_ref, *refs):
        for k in range(4):
            refs[4][:, k] = refs[3 - k][...]

    return call(
        body, "stack_pieces", SHORT, shape(16, 4, 32, 128), pieces[::-1], [], 1,
        near=0, out_near=True,
    )


def change_rows(average, m_rows):
    def body(rg_ref, avg_ref, m_ref, o_ref, avg, m, o, sems):
        flip = jnp.where(peer(rg_ref[0], rg_ref[1]) == 3, 4, 0)
        copies = Copies(sems)
        loads = [
            (
                copies.start(avg_ref.at[:, pl.ds(p * WIDTH, WIDTH)], avg.at[p]),
                copies.start(m_ref.at[pl.ds(p * 16, 16)], m.at[p]),
            )
            for p in range(PARTS)
        ]
        for p in range(PARTS):
            for load in loads[p]:
                load.wait()

            def step(n, carry, p=p):
                cols = at(n * 128, 128)
                x = avg[p, :, cols]
                momentum = outer_beta * m[p, peer(n, flip)].astype(F32) + x
                o[p, :, cols] = (outer_rate * (x + outer_beta * momentum)).astype(BF)
                return carry

            lax.fori_loop(0, 16, step, 0, unroll=4)
            copies.send(o.at[p], o_ref.at[:, pl.ds(p * WIDTH, WIDTH)])
        copies.finish()

    return call(
        body, "change_rows", SHORT, shape(32, 8192), [average, m_rows],
        [shape(PARTS, 32, WIDTH, dtype=F32), shape(4, 16, 32, 128), shape(PARTS, 32, WIDTH)],
        3 * PARTS,
    )


def new_momentum_of(momentum, pieces, after):
    def body(rg_ref, after_ref, p_ref, m_ref, o_ref, q, o, sems):
        copies = Copies(sems)
        loads = [copies.start(p_ref.at[pl.ds(8 * i, 8)], q.at[pl.ds(8 * i, 8)]) for i in range(2)]
        r, g = rg_ref[0], rg_ref[1]
        for p in range(4):
            if p % 2 == 0:
                loads[p // 2].wait()
            for k in range(4):
                other = peer(g, k)
                flip = jnp.where(other // 2 == r // 2, 0, 4)
                for j in range(4):
                    rows = at(j * 128 + seg_of(other) * 32, 32)
                    all_rows = at((4 * p + j) * 128 + seg_of(other) * 32, 32)
                    piece = q[peer(4 * p + j, flip), k].astype(F32)
                    o[p, rows, :] = outer_beta * m_ref[all_rows, :] + piece
            copies.send(o.at[p], o_ref.at[pl.ds(p * 512, 512), :])
        copies.finish()

    return call(
        body, "new_momentum_of", SHORT, shape(2048, 128, dtype=F32),
        [after, pieces, momentum], [shape(16, 4, 32, 128), shape(4, 512, 128, dtype=F32)], 6,
        near=2,
    )


def outputs_of(local, anchor, changes, before):
    ks = sorted(changes)
    n = len(ks)

    def body(r_ref, l_ref, a_ref, *refs):
        new_ref, mixed_ref, l, a, c, new, mixed, sems = refs[-8:]
        copies = Copies(sems)
        loads = []
        for m, k in enumerate(ks):
            rows = at(seg_of(peer(r_ref[0], k)) * 32, 32)
            for p in range(PARTS):
                cols = pl.ds(p * WIDTH, WIDTH)
                i = m * PARTS + p
                loads.append((
                    rows,
                    cols,
                    copies.start(l_ref.at[rows, cols], l.at[i]),
                    copies.start(a_ref.at[rows, cols], a.at[i]),
                    copies.start(refs[m].at[:, cols], c.at[i]),
                ))
        for i, (rows, cols, *waits) in enumerate(loads):
            for load in waits:
                load.wait()

            def step(x, i=i):
                global_new = a[i, :, x].astype(F32) - c[i, :, x].astype(F32)
                new[i, :, x] = global_new.astype(BF)
                mixed[i, :, x] = (
                    mix_weight * l[i, :, x].astype(F32) + (1.0 - mix_weight) * global_new
                ).astype(BF)

            inner(step)
            copies.send(new.at[i], new_ref.at[rows, cols])
            copies.send(mixed.at[i], mixed_ref.at[rows, cols])
        copies.finish()

    return call(
        body, "outputs_of", SHORT, [shape(128, 8192)] * 2,
        [local, anchor, *[changes[k] for k in ks], *before],
        [shape(n * PARTS, 32, WIDTH)] * 5, 5 * n * PARTS,
        {2 + n + b: b for b in range(len(before))},
    )


def across(x, k):
    pairs = [
        (64 * r + 16 * g + q, 64 * g + 16 * (r ^ k) + (q if r // 2 == g // 2 else q ^ 4))
        for r in range(4)
        for g in range(4)
        for q in range(16)
    ]
    return lax.ppermute(x, ("replica", "fsdp"), pairs)


def in_hbm(x):
    return pltpu.with_memory_space_constraint(x, pltpu.HBM)


def local(local_weights, anchor, momentum):
    own, anchor = in_hbm(local_weights[0]), in_hbm(anchor)

    half, *pieces = prologue(own, in_hbm(momentum))
    theirs = swap(half, 1)
    pieces = [pieces[0], swap(pieces[1], 1), swap(pieces[2], 2), swap_around(pieces[3])]
    mine, for_other = partial_rows(own, theirs, anchor)
    partial = swap(for_other, 2)
    by_row = in_order(pieces, for_other).reshape(64, 32, 128)
    m_rows = lax.all_to_all(by_row, "fsdp", 0, 0, tiled=True)

    average, *cut = average_rows(mine, partial)
    cut = stack_pieces([across(x, k) for k, x in enumerate(cut)])
    groups = [[16 * i + q for q in range(16)] for i in range(4)]
    cut = lax.all_to_all(cut, "fsdp", 0, 0, axis_index_groups=groups, tiled=True)

    change = change_rows(average, m_rows)
    change2 = swap(change, 2)
    change1 = swap(change, 1)
    change3 = swap(change2, 1)
    outs = outputs_of(own, anchor, {0: change, 1: change1}, ())
    outs = outputs_of(own, anchor, {2: change2}, outs)
    new_anchor, mixed = outputs_of(own, anchor, {3: change3}, outs)
    new_momentum = new_momentum_of(momentum, cut, in_hbm(mixed))
    return new_momentum, new_anchor, mixed[None]


def solution(mesh):
    return jax.shard_map(
        local,
        mesh=mesh,
        in_specs=(P("replica", "fsdp", None), P("fsdp", None), P("replica", "fsdp")),
        out_specs=(P("replica", "fsdp"), P("fsdp", None), P("replica", "fsdp", None)),
        check_vma=False,
    )
```

```python
import jax
import jax.numpy as jnp
from jax import lax
from jax.experimental import pallas as pl
from jax.experimental.pallas import tpu as pltpu
from jax.sharding import PartitionSpec as P

outer_rate = 0.7
outer_beta = 0.9
mix_weight = 0.5

BF = jnp.bfloat16
F32 = jnp.float32
PARTS = 4
WIDTH = 8192 // PARTS
INNER = 512
SHORT = 2 << 20
LONG = 1 << 34
VMEM_MIB = 16


def seg_of(r):
    return 2 * (r % 2) + r // 2


def peer(r, k):
    return jnp.bitwise_xor(r, k)


def shape(*dims, dtype=BF):
    return jax.ShapeDtypeStruct(dims, dtype)


def at(start, count):
    return pl.ds(pl.multiple_of(start, count), count)


class Copies:
    def __init__(self, sems):
        self.sems, self.count, self.open = sems, 0, []

    def start(self, src, dst):
        copy = pltpu.make_async_copy(src, dst, self.sems.at[self.count])
        copy.start()
        self.count += 1
        return copy

    def send(self, src, dst):
        self.open.append(self.start(src, dst))

    def finish(self):
        for copy in self.open:
            copy.wait()


class Place:
    def __getitem__(self, i):
        return lax.axis_index("fsdp") // 16 if i else lax.axis_index("replica")


def call(body, name, cost, outs, args, scratch, copies, aliases=None, near=None, out_near=False,
         far=0):
    anywhere = pl.BlockSpec(memory_space=pl.ANY)
    whole = pl.BlockSpec(memory_space=pltpu.VMEM)
    near = len(args) if near is None else near
    out_spec = whole if out_near else anywhere
    single = not isinstance(outs, list)
    count = 1 if single else len(outs)
    return pl.pallas_call(
        lambda *refs: body(Place(), *refs),
        out_shape=outs,
        in_specs=[anywhere] * near + [whole] * (len(args) - near),
        out_specs=out_spec if single else [anywhere] * far + [out_spec] * (count - far),
        scratch_shapes=[pltpu.VMEM(x.shape, x.dtype) for x in scratch]
        + [pltpu.SemaphoreType.DMA((copies,))],
        input_output_aliases=aliases or {},
        compiler_params=pltpu.CompilerParams(vmem_limit_bytes=VMEM_MIB * 2**20),
        cost_estimate=pl.CostEstimate(flops=cost, bytes_accessed=cost, transcendentals=0),
        name=name,
    )(*args)


def swap(x, k):
    return lax.ppermute(x, "replica", [(i, i ^ k) for i in range(4)])


def swap_around(x):
    pairs = [(64 * i + f, 64 * (i ^ 3) + (f ^ 4)) for i in range(4) for f in range(64)]
    return lax.ppermute(x, ("replica", "fsdp"), pairs)


def prologue(local, momentum):
    def body(r_ref, l_ref, m_ref, half_ref, *refs):
        outs, (m, sems) = refs[:4], refs[4:]
        copies = Copies(sems)
        loads = [
            copies.start(m_ref.at[pl.ds(p * 512, 512), :], m.at[pl.ds(p * 512, 512), :])
            for p in range(4)
        ]
        other = 1 - r_ref[0] % 2
        copies.send(l_ref.at[at(other * 64, 64), :], half_ref)
        for p in range(4):
            loads[p].wait()
            for k in range(4):
                seg = seg_of(peer(r_ref[0], k))
                for j in range(4 * p, 4 * p + 4):
                    outs[k][j] = m[at(j * 128 + seg * 32, 32), :].astype(BF)
        copies.finish()

    return call(
        body, "prologue", SHORT, [shape(64, 8192)] + [shape(16, 32, 128)] * 4,
        [local, momentum], [shape(2048, 128, dtype=F32)], 5, out_near=True,
    )


def in_order(pieces, after):
    def body(r_ref, after_ref, *refs):
        for k in range(4):
            refs[4][peer(r_ref[0], k)] = refs[3 - k][...]

    return call(
        body, "in_order", LONG, shape(4, 16, 32, 128), [after, *pieces[::-1]], [], 1,
        near=1, out_near=True,
    )


def inner(step):
    lax.fori_loop(
        0, WIDTH // INNER, lambda i, c: (step(at(i * INNER, INNER)), c)[1], 0, unroll=True
    )


def partial_rows(local, theirs, anchor):
    def body(r_ref, l_ref, t_ref, a_ref, own_ref, other_ref, l, t, a, own, sems):
        copies = Copies(sems)
        loads = []
        for k in (2, 0):
            device = peer(r_ref[0], k)
            mine = at(seg_of(device) * 32, 32)
            half = at((device // 2) * 32, 32)
            for p in range(PARTS):
                cols = pl.ds(p * WIDTH, WIDTH)
                i = len(loads)
                loads.append([
                    copies.start(l_ref.at[mine, cols], l.at[i]),
                    copies.start(t_ref.at[half, cols], t.at[i]),
                    copies.start(a_ref.at[mine, cols], a.at[i]),
                ])
        for i, waits in enumerate(loads):
            for load in waits:
                load.wait()
            p = i % PARTS

            def step(n, carry, i=i, p=p):
                cols = at(n * INNER, INNER)
                x = a[i, :, cols].astype(F32)
                total = (x - l[i, :, cols].astype(F32)) + (x - t[i, :, cols].astype(F32))
                if i < PARTS:
                    other_ref[:, at(p * WIDTH + n * INNER, INNER)] = total.astype(BF)
                else:
                    own[p, :, cols] = total.astype(BF)
                return carry

            lax.fori_loop(0, WIDTH // INNER, step, 0, unroll=True)
            if i >= PARTS:
                copies.send(own.at[p], own_ref.at[:, pl.ds(p * WIDTH, WIDTH)])
        copies.finish()

    return call(
        body, "partial_rows", SHORT, [shape(32, 8192)] * 2,
        [local, theirs, anchor],
        [shape(2 * PARTS, 32, WIDTH)] * 3
        + [shape(PARTS, 32, WIDTH)],
        7 * PARTS, out_near=True, far=1,
    )


def average_rows(own, partial):
    def body(r_ref, own_ref, p_ref, avg_ref, *refs):
        outs, (x, q, avg, sems) = refs[:4], refs[4:]
        copies = Copies(sems)
        loads = []
        for k in range(4):
            cols = at(peer(r_ref[0], k) * WIDTH, WIDTH)
            loads.append([
                copies.start(own_ref.at[:, cols], x.at[k]),
                copies.start(p_ref.at[:, cols], q.at[k]),
            ])
        for k in range(4):
            for load in loads[k]:
                load.wait()

            def step(i, carry, k=k):
                cols = at(i * INNER, INNER)
                y = (x[k, :, cols].astype(F32) + q[k, :, cols].astype(F32)) * 0.25
                narrow = y.astype(BF)
                avg[k, :, cols] = narrow
                for n in range(INNER // 128):
                    outs[k][i * (INNER // 128) + n] = narrow[:, n * 128 : (n + 1) * 128]
                return carry

            lax.fori_loop(0, WIDTH // INNER, step, 0, unroll=True)
            copies.send(avg.at[k], avg_ref.at[:, at(peer(r_ref[0], k) * WIDTH, WIDTH)])
        copies.finish()

    return call(
        body, "average_rows", LONG, [shape(32, 8192)] + [shape(16, 32, 128)] * 4,
        [own, partial],
        [shape(4, 32, WIDTH)] * 3, 12, out_near=True, far=1,
    )


def stack_pieces(pieces):
    def body(r_ref, *refs):
        for k in range(4):
            refs[4][:, k] = refs[3 - k][...]

    return call(
        body, "stack_pieces", SHORT, shape(16, 4, 32, 128), pieces[::-1], [], 1,
        near=0, out_near=True,
    )


def change_rows(average, m_rows):
    def body(rg_ref, avg_ref, m_ref, o_ref, avg, m, o, sems):
        flip = jnp.where(peer(rg_ref[0], rg_ref[1]) == 3, 4, 0)
        copies = Copies(sems)
        loads = [
            (
                copies.start(avg_ref.at[:, pl.ds(p * WIDTH, WIDTH)], avg.at[p]),
                copies.start(m_ref.at[pl.ds(p * 16, 16)], m.at[p]),
            )
            for p in range(PARTS)
        ]
        for p in range(PARTS):
            for load in loads[p]:
                load.wait()

            def step(n, carry, p=p):
                cols = at(n * 128, 128)
                x = avg[p, :, cols].astype(F32)
                momentum = outer_beta * m[p, peer(n, flip)].astype(F32) + x
                o[p, :, cols] = (outer_rate * (x + outer_beta * momentum)).astype(BF)
                return carry

            lax.fori_loop(0, 16, step, 0, unroll=4)
            copies.send(o.at[p], o_ref.at[:, pl.ds(p * WIDTH, WIDTH)])
        copies.finish()

    return call(
        body, "change_rows", SHORT, shape(32, 8192), [average, m_rows],
        [shape(PARTS, 32, WIDTH), shape(4, 16, 32, 128), shape(PARTS, 32, WIDTH)],
        3 * PARTS,
    )


def new_momentum_of(momentum, pieces, after):
    def body(rg_ref, after_ref, p_ref, m_ref, o_ref, q, o, sems):
        copies = Copies(sems)
        loads = [copies.start(p_ref.at[pl.ds(8 * i, 8)], q.at[pl.ds(8 * i, 8)]) for i in range(2)]
        r, g = rg_ref[0], rg_ref[1]
        for p in range(4):
            if p % 2 == 0:
                loads[p // 2].wait()
            for k in range(4):
                other = peer(g, k)
                flip = jnp.where(other // 2 == r // 2, 0, 4)
                for j in range(4):
                    rows = at(j * 128 + seg_of(other) * 32, 32)
                    all_rows = at((4 * p + j) * 128 + seg_of(other) * 32, 32)
                    piece = q[peer(4 * p + j, flip), k].astype(F32)
                    o[p, rows, :] = outer_beta * m_ref[all_rows, :] + piece
            copies.send(o.at[p], o_ref.at[pl.ds(p * 512, 512), :])
        copies.finish()

    return call(
        body, "new_momentum_of", SHORT, shape(2048, 128, dtype=F32),
        [after, pieces, momentum], [shape(16, 4, 32, 128), shape(4, 512, 128, dtype=F32)], 6,
        near=2,
    )


def outputs_of(local, anchor, changes, before):
    ks = sorted(changes)
    n = len(ks)

    def body(r_ref, l_ref, a_ref, *refs):
        new_ref, mixed_ref, l, a, c, new, mixed, sems = refs[-8:]
        copies = Copies(sems)
        loads = []
        for m, k in enumerate(ks):
            rows = at(seg_of(peer(r_ref[0], k)) * 32, 32)
            for p in range(PARTS):
                cols = pl.ds(p * WIDTH, WIDTH)
                i = m * PARTS + p
                loads.append((
                    rows,
                    cols,
                    copies.start(l_ref.at[rows, cols], l.at[i]),
                    copies.start(a_ref.at[rows, cols], a.at[i]),
                    copies.start(refs[m].at[:, cols], c.at[i]),
                ))
        for i, (rows, cols, *waits) in enumerate(loads):
            for load in waits:
                load.wait()

            def step(x, i=i):
                global_new = a[i, :, x].astype(F32) - c[i, :, x].astype(F32)
                new[i, :, x] = global_new.astype(BF)
                mixed[i, :, x] = (
                    mix_weight * l[i, :, x].astype(F32) + (1.0 - mix_weight) * global_new
                ).astype(BF)

            inner(step)
            copies.send(new.at[i], new_ref.at[rows, cols])
            copies.send(mixed.at[i], mixed_ref.at[rows, cols])
        copies.finish()

    return call(
        body, "outputs_of", SHORT, [shape(128, 8192)] * 2,
        [local, anchor, *[changes[k] for k in ks], *before],
        [shape(n * PARTS, 32, WIDTH)] * 5, 5 * n * PARTS,
        {2 + n + b: b for b in range(len(before))},
    )


def across(x, k):
    pairs = [
        (64 * r + 16 * g + q, 64 * g + 16 * (r ^ k) + (q if r // 2 == g // 2 else q ^ 4))
        for r in range(4)
        for g in range(4)
        for q in range(16)
    ]
    return lax.ppermute(x, ("replica", "fsdp"), pairs)


def in_hbm(x):
    return pltpu.with_memory_space_constraint(x, pltpu.HBM)


def local(local_weights, anchor, momentum):
    own, anchor = in_hbm(local_weights[0]), in_hbm(anchor)

    half, *pieces = prologue(own, in_hbm(momentum))
    theirs = swap(half, 1)
    pieces = [pieces[0], swap(pieces[1], 1), swap(pieces[2], 2), swap_around(pieces[3])]
    mine, for_other = partial_rows(own, theirs, anchor)
    partial = swap(for_other, 2)
    by_row = in_order(pieces, for_other).reshape(64, 32, 128)
    m_rows = lax.all_to_all(by_row, "fsdp", 0, 0, tiled=True)

    average, *cut = average_rows(mine, partial)
    cut = stack_pieces([across(x, k) for k, x in enumerate(cut)])
    groups = [[16 * i + q for q in range(16)] for i in range(4)]
    cut = lax.all_to_all(cut, "fsdp", 0, 0, axis_index_groups=groups, tiled=True)

    change = change_rows(average, m_rows)
    change2 = swap(change, 2)
    change1 = swap(change, 1)
    change3 = swap(change2, 1)
    outs = outputs_of(own, anchor, {0: change, 1: change1}, ())
    outs = outputs_of(own, anchor, {2: change2}, outs)
    new_anchor, mixed = outputs_of(own, anchor, {3: change3}, outs)
    new_momentum = new_momentum_of(momentum, cut, in_hbm(mixed))
    return new_momentum, new_anchor, mixed[None]


def solution(mesh):
    return jax.shard_map(
        local,
        mesh=mesh,
        in_specs=(P("replica", "fsdp", None), P("fsdp", None), P("replica", "fsdp")),
        out_specs=(P("replica", "fsdp"), P("fsdp", None), P("replica", "fsdp", None)),
        check_vma=False,
    )
```
